512 devices in a mesh: dp: 4 (over z_hi), tm: 64 (over x, y, z_lo), space: 2 (over core).
Axes of the slice: x: 4, y: 4, z: 16 (z_hi: 4, z_lo: 4; z = z_hi * 4 + z_lo), core: 2. Of those that a mesh axis runs over, the one named last changes fastest.
Arguments:
- inputs: bfloat16 [4, 128, 16, 32, 128], P('dp', 'tm', 'space'), may hold values from -6 to 6
- clip_lengths: int32 [4, 4], P('dp'), may hold values from 1 to 64, 128 in all within a row
- weight: bfloat16 [3, 3, 3, 128, 128], replicated, may hold values from -0.109375 to 0.109375
- bias: float32 [128], replicated, may hold values from -3 to 3
- cotangent: bfloat16 [4, 128, 16, 32, 128], P('dp', 'tm', 'space'), may hold values from -6 to 6
Outputs:
- outputs: bfloat16 [4, 128, 16, 32, 128], P('dp', 'tm', 'space')
- input_grad: bfloat16 [4, 128, 16, 32, 128], P('dp', 'tm', 'space')
- weight_grad: float32 [3, 3, 3, 128, 128], replicated
- bias_grad: float32 [128], replicated
The draws below stay inside these ranges and needn't reach their ends.
Inputs may be any that keep to these rules, and one draw needn't show every extreme that they name: `clip_lengths`: each row sums to 128 and its largest entry is exactly 64.
All inputs are finite; a program needn't handle non-finite values.
Results may differ from the reference program's by a relative error of at most 0.008.
Values may be sent and summed in bfloat16 or wider, within the bound.
A program may use at most 64 MiB of HBM per device.

```python
import math
import jax
import jax.numpy as jnp
import numpy as np
from jax import lax

C = 128
COLS = 32
CLIPS = 4
PACKS = 4
FRAMES = 128
ROWS = 16
MOST_LEN = 64


def level_of(own_key, dims, shards, smallest, largest):
    level, own = 1.0, jax.random.fold_in(own_key, 6)
    for axis_at, shards_of in shards:
        steps = jnp.exp(jax.random.uniform(jax.random.fold_in(own, axis_at), (shards_of,), jnp.float32, smallest / len(shards), largest / len(shards)))
        level = level * jnp.repeat(steps, dims[axis_at] // shards_of).reshape([-1 if axis == axis_at else 1 for axis in range(len(dims))])
    return level


def length_profile(number_of, total, most, lean):
    loads = [(1 << 20) // math.isqrt(standing ** lean) + 1 for standing in range(2, number_of + 1)]
    spare, holding = total - most - (number_of - 1), [1] * (number_of - 1)
    while spare > 0:
        candidates = [i for i in range(number_of - 1) if holding[i] < most]
        mass, left = sum([loads[i] for i in candidates]), spare
        for i in candidates:
            addition = min(most - holding[i], max(1, left * loads[i] // mass), spare)
            holding[i] = holding[i] + addition
            spare = spare - addition
    return np.array([most] + holding)


def uneven_parts(stream_key, amount, total, bound, slope):
    if amount == 2:
        one = jax.random.randint(stream_key, (), max(1, total - bound), min(bound, total - 1) + 1)
        return jnp.stack([one, total - one])
    tallies = jnp.asarray(length_profile(amount, total, bound, slope), jnp.int32)
    twos = (amount - 1) // 2
    donor, sink = tallies[1:1 + 2 * twos:2], tallies[2:2 + 2 * twos:2]
    slack = jnp.minimum(donor - 1, bound - sink)
    moved = jax.random.randint(jax.random.fold_in(stream_key, 1), (twos,), 0, 1 << 20) % (slack + 1)
    tallies = tallies.at[1:1 + 2 * twos:2].set(donor - moved).at[2:2 + 2 * twos:2].set(sink + moved)
    return tallies[jax.random.permutation(jax.random.fold_in(stream_key, 2), amount)]


def scatter_about(rng, extent, spread, reach, cuts=(), kind=jnp.bfloat16):
    entries = jax.random.normal(rng, extent, jnp.float32) * spread
    if len(cuts) > 0:
        entries = level_of(rng, extent, cuts, -0.22, 0.18) * entries
    return jnp.clip(entries, min=-reach, max=reach).astype(kind)


def setup_inputs(seed: int = 0) -> dict:
    arg_keys = jax.random.split(jax.random.key(seed), 6)
    return {
        "inputs": scatter_about(arg_keys[0], (PACKS, FRAMES, ROWS, COLS, C), 1.0, 6.0, ((0, 4), (1, 64), (2, 2))),
        "clip_lengths": jax.vmap(lambda own: uneven_parts(own, CLIPS, FRAMES, MOST_LEN, 2))(jax.random.split(arg_keys[1], PACKS)).reshape((PACKS, CLIPS)).astype(jnp.int32),
        "weight": scatter_about(arg_keys[2], (3, 3, 3, C, C), (27 * C) ** -0.5, 0.109375),
        "bias": scatter_about(arg_keys[3], (C,), 0.5, 3.0, (), jnp.float32),
        "cotangent": scatter_about(arg_keys[4], (PACKS, FRAMES, ROWS, COLS, C), 1.0, 6.0, ((0, 4), (1, 64), (2, 2))),
    }


def clip_index(lengths, frames):
    ends = jnp.cumsum(lengths).astype(jnp.int32)
    return lax.optimization_barrier(jnp.sum((frames[:, None] >= ends[None, :]).astype(jnp.int32), axis=1))

def tap_masks(lengths, frames):
    own = clip_index(lengths, frames)
    rows = []
    for k in range(3):
        earlier = frames - (2 - k)
        keep = (earlier >= 0) & (clip_index(lengths, earlier) == own)
        rows.append(keep.astype(jnp.float32))
    return jnp.stack(rows)

def linear_part(values, kernel, masks):
    padded = jnp.pad(values, ((2, 0), (0, 0), (0, 0), (0, 0)))
    total = jnp.zeros(values.shape, jnp.float32)
    for k in range(3):
        source = padded[k:k + FRAMES]
        out = lax.conv_general_dilated(source, kernel[k], (1, 1), ((1, 1), (1, 1)), dimension_numbers=('NHWC', 'HWIO', 'NHWC'), precision=lax.Precision.HIGHEST)
        total = total + masks[k][:, None, None, None] * out
    return total

def reference(inputs, clip_lengths, weight, bias, cotangent):
    kernel = weight.astype(jnp.float32)

    def one_pack(items):
        values, grads, lengths = items
        frames = jnp.arange(FRAMES, dtype=jnp.int32)
        masks = tap_masks(lengths, frames)
        flat_in = values.astype(jnp.float32)
        z = linear_part(flat_in, kernel, masks) + bias.astype(jnp.float32)
        sig = jax.nn.sigmoid(z)
        result = (z * sig).astype(jnp.bfloat16)
        dz = (grads.astype(jnp.float32) * sig * (1.0 + z * (1.0 - sig))).astype(jnp.bfloat16)
        _, pull = jax.vjp(lambda left, right: linear_part(left, right, masks), flat_in, kernel)
        in_grad, kern_grad = pull(dz.astype(jnp.float32))
        return (result, in_grad.astype(jnp.bfloat16), kern_grad, lax.optimization_barrier(jnp.sum(dz.astype(jnp.float32), axis=(0, 1, 2))))
    result, in_grad, kern_grad, bias_terms = lax.map(one_pack, (inputs, cotangent, clip_lengths))
    return (result, in_grad, lax.optimization_barrier(jnp.sum(kern_grad, axis=0)), lax.optimization_barrier(jnp.sum(bias_terms, axis=0)))
```

```python
import functools

import jax
import jax.numpy as jnp
from jax import lax
from jax.experimental import pallas as pl
from jax.experimental.pallas import tpu as pltpu
from jax.sharding import PartitionSpec as P

MESH = pl.DeviceIdType.MESH
Z_LO = 4
HALF = 64
ROWS = 28 * HALF
BIAS_ROW = 27 * HALF


def scalar_mask(ends, frame, lag):
    def clip(t):
        return sum((t >= end).astype(jnp.int32) for end in ends)

    earlier = frame - lag
    same = (clip(earlier) == clip(frame)) & (earlier >= 0)
    return same.astype(jnp.float32)


def scaled(values, mask):
    return values * jnp.full(values.shape, mask, jnp.float32).astype(values.dtype)


def column_sum(parts, back):
    count = parts.shape[0]
    col = lax.broadcasted_iota(jnp.int32, (count, 128), 0) % 32
    first, mid, last = parts[:, :128], parts[:, 128:256], parts[:, 256:]
    down, up = (last, first) if back else (first, last)
    down = jnp.where(col == 0, 0.0, pltpu.roll(down, 1, 0))
    up = jnp.where(col == 31, 0.0, pltpu.roll(up, count - 1, 0))
    return mid + down + up


def chip_kernel(
    dims, lens, x_hbm, w_hbm, bias_ref, cot_hbm,
    out_ref, ig_ref, full,
    xs, xt, lt, dzs, wv, cotv, yacc, part, rsbuf, zs, zbuf,
    loc, xsend, xrecv, dsend, drecv, rs_send, rs_recv, z_send, z_recv,
    zg_send, zg_recv, pg_send, pg_recv, cg_send, cg_recv,
):
    zh_n, tm_n = dims
    z_n, p_n = zh_n * Z_LO, tm_n // Z_LO
    chunk = ROWS // p_n
    tiles = chunk // 16
    group = max(1, tiles // z_n)
    owners = tiles // group
    stride = z_n // owners
    piece = group * 16

    dp, tm, core = lax.axis_index("dp"), lax.axis_index("tm"), lax.axis_index("space")
    other = 1 - core
    p, zl = tm // Z_LO, tm % Z_LO
    z = dp * Z_LO + zl
    after, before = (tm + 1) % tm_n, (tm + tm_n - 1) % tm_n

    def plane_dev(q):
        return (dp, q * Z_LO + zl, core)

    def z_dev(w):
        return (w // Z_LO, p * Z_LO + w % Z_LO, core)

    barrier = pltpu.get_barrier_semaphore()

    def greet(device):
        pl.semaphore_signal(barrier, inc=1, device_id=device, device_id_type=MESH)

    def remote(src, dst, send, recv, device):
        return pltpu.make_async_remote_copy(
            src_ref=src, dst_ref=dst, send_sem=send, recv_sem=recv, device_id=device, device_id_type=MESH
        )

    own = pl.ds(1 + 8 * core, 8)
    edge_row = 7 * other
    edge = pl.ds(1 + 8 * core + edge_row, 1)
    inner = pl.ds(1 + 9 * core, 7)

    for f in range(4):
        for r in (0, 17):
            xs[f, r] = jnp.zeros((32, 128), jnp.bfloat16)
            dzs[f, r] = jnp.zeros((32, 128), jnp.bfloat16)
    get_x = pltpu.make_async_copy(x_hbm.at[0], xs.at[pl.ds(2, 2), own], loc.at[0])
    get_w = pltpu.make_async_copy(w_hbm, wv, loc.at[1])
    get_cot = pltpu.make_async_copy(cot_hbm.at[0], cotv, loc.at[2])
    get_x.start()
    get_w.start()
    get_cot.start()

    greet((dp, tm, other))
    for near in (before, after):
        greet((dp, near, core))
        greet((dp, near, other))
    pl.loop(1, p_n)(lambda i: greet(plane_dev((p + i) % p_n)))
    pl.loop(1, z_n)(lambda i: greet(z_dev((z + i) % z_n)))
    pl.semaphore_wait(barrier, 5 + p_n - 1 + z_n - 1)

    x_next = remote(x_hbm.at[0], xs.at[pl.ds(0, 2), own], xsend.at[1], xrecv.at[1], (dp, after, core))
    x_edge = remote(
        x_hbm.at[0, pl.ds(0, 2), pl.ds(edge_row, 1)], xs.at[pl.ds(0, 2), edge],
        xsend.at[2], xrecv.at[2], (dp, after, other),
    )
    x_pair = remote(x_hbm.at[0], xs.at[pl.ds(2, 2), own], xsend.at[0], xrecv.at[0], (dp, tm, other))
    x_fwd = remote(
        xs.at[pl.ds(0, 2), inner], xs.at[pl.ds(0, 2), inner], xsend.at[3], xrecv.at[3], (dp, tm, other)
    )
    x_next.start()
    x_edge.start()
    x_pair.start()

    ends = [lens[0, 0]]
    for j in range(1, lens.shape[1]):
        ends.append(ends[-1] + lens[0, j])
    base = 2 * tm
    m0 = [scalar_mask(ends, base + t, 2) for t in range(4)]
    m1 = [scalar_mask(ends, base + t, 1) for t in range(3)]

    def x_rows(f):
        return jnp.concatenate(
            [xs[f, pl.ds(8 * core + a, 8)].reshape(256, 128) for a in range(3)], axis=1
        )

    def w_fwd(k):
        return jnp.concatenate(
            [jnp.concatenate([wv[k, a, b] for b in range(3)], axis=1) for a in range(3)], axis=0
        )

    def mm(lhs, rhs):
        return jnp.dot(lhs, rhs, preferred_element_type=jnp.float32)

    def turned(f):
        xt[...] = xs[f, pl.ds(1, 16)].reshape(512, 128).astype(jnp.float32).T
        mid = xt[pl.ds(pl.multiple_of(HALF * core, HALF), HALF), :]
        col = lax.broadcasted_iota(jnp.int32, (HALF, 512), 1) % 32
        left = jnp.where(col == 0, 0.0, pltpu.roll(mid, 1, 1))
        right = jnp.where(col == 31, 0.0, pltpu.roll(mid, 511, 1))
        block = jnp.concatenate([left, mid, right], axis=0)
        for t in range(2):
            k = f - t
            if k < 0 or k > 2:
                continue
            kept = block if k == 2 else block * (m1[t] if k == 1 else m0[t])
            lt[k, :, pl.ds(512 * t, 512)] = kept.astype(jnp.bfloat16)

    get_x.wait()
    get_w.wait()
    x_pair.wait_recv()
    yacc[0] = mm(x_rows(2), w_fwd(2))
    yacc[1] = mm(
        jnp.concatenate([x_rows(3), scaled(x_rows(2), m1[1])], axis=1),
        jnp.concatenate([w_fwd(2), w_fwd(1)], axis=0),
    )
    turned(2)
    turned(3)
    get_cot.wait()

    x_next.wait_recv()
    x_fwd.start()
    x_edge.wait_recv()
    yacc[0] += mm(
        jnp.concatenate([scaled(x_rows(1), m1[0]), scaled(x_rows(0), m0[0])], axis=1),
        jnp.concatenate([w_fwd(1), w_fwd(0)], axis=0),
    )
    yacc[1] += mm(scaled(x_rows(1), m0[1]), w_fwd(0))

    bias_part = jnp.zeros((16, 128), jnp.float32)
    for f in range(2):
        zed = column_sum(yacc[f], False) + bias_ref[...]
        sig = jax.nn.sigmoid(zed)
        out_ref[0, f] = (zed * sig).astype(jnp.bfloat16).reshape(8, 32, 128)
        cot = cotv[f].reshape(256, 128).astype(jnp.float32)
        dz = (cot * sig * (1.0 + zed * (1.0 - sig))).astype(jnp.bfloat16)
        dzs[f, own] = dz.reshape(8, 32, 128)
        bias_part += jnp.sum(dz.astype(jnp.float32).reshape(16, 16, 128), axis=0)

    two, later = pl.ds(0, 2), pl.ds(2, 2)
    d_pair = remote(dzs.at[two, own], dzs.at[two, own], dsend.at[0], drecv.at[0], (dp, tm, other))
    d_next = remote(dzs.at[two, own], dzs.at[later, own], dsend.at[1], drecv.at[1], (dp, before, core))
    d_edge = remote(dzs.at[two, edge], dzs.at[later, edge], dsend.at[2], drecv.at[2], (dp, before, other))
    d_pair.start()
    d_next.start()
    d_edge.start()

    part[pl.ds(BIAS_ROW, 16), :] = bias_part.astype(jnp.bfloat16)
    part[pl.ds(BIAS_ROW + 16, ROWS - BIAS_ROW - 16), :] = jnp.zeros((ROWS - BIAS_ROW - 16, 128), jnp.bfloat16)
    x_fwd.wait_recv()
    turned(0)
    turned(1)
    d_pair.wait_recv()

    right_side = jnp.concatenate(
        [
            jnp.concatenate([dzs[t, pl.ds(2 - a, 16)].reshape(512, 128) for a in range(3)], axis=1)
            for t in range(2)
        ],
        axis=0,
    )

    def chunk_rows(q):
        return pl.ds(pl.multiple_of(q * chunk, 16), chunk)

    def rs_copy(q):
        return remote(
            part.at[chunk_rows(q)], rsbuf.at[p], rs_send.at[q], rs_recv.at[p], plane_dev(q)
        )

    def rs_start(q):
        @pl.when(q != p)
        def _():
            rs_copy(q).start()

    sent = 0
    for k in range(3):
        grad = mm(lt[k], right_side)
        for a in range(3):
            for b in range(3):
                tap = (k * 3 + a) * 3 + b
                part[pl.ds(tap * HALF, HALF), :] = grad[
                    b * HALF : (b + 1) * HALF, a * 128 : (a + 1) * 128
                ].astype(jnp.bfloat16)
        ready = p_n if k == 2 else (k + 1) * 9 * HALF // chunk
        pl.loop(sent, ready)(rs_start)
        sent = ready
    rsbuf[pl.ds(p, 1)] = part[chunk_rows(p), :][None]

    def d_rows(f):
        return jnp.concatenate(
            [dzs[f, pl.ds(8 * core + 2 - a, 8)].reshape(256, 128) for a in range(3)], axis=1
        )

    def w_back(k):
        return jnp.concatenate([wv[k, a].reshape(384, 128) for a in range(3)], axis=1)

    def mm_t(lhs, rhs):
        return lax.dot_general(lhs, rhs, (((1,), (1,)), ((), ())), preferred_element_type=jnp.float32)

    yacc[0] = mm_t(
        jnp.concatenate([d_rows(0), scaled(d_rows(1), m1[1])], axis=1),
        jnp.concatenate([w_back(2), w_back(1)], axis=1),
    )
    yacc[1] = mm_t(d_rows(1), w_back(2))

    @pl.loop(1, p_n)
    def _(i):
        q = (p + i) % p_n
        remote(part.at[chunk_rows(q)], rsbuf.at[q], rs_send.at[q], rs_recv.at[q], plane_dev(q)).wait_recv()

    total = rsbuf[0].astype(jnp.float32)
    for q in range(1, p_n):
        total += rsbuf[q].astype(jnp.float32)
    zs[...] = total.astype(jnp.bfloat16)

    phase = core % stride

    def owner_of(j):
        return stride * j + phase

    def z_copy(j):
        return remote(
            zs.at[pl.ds(pl.multiple_of(j * piece, 16), piece)], zbuf.at[z], z_send.at[j], z_recv.at[z],
            z_dev(owner_of(j)),
        )

    @pl.loop(0, owners)
    def _(j):
        @pl.when(owner_of(j) != z)
        def _():
            z_copy(j).start()

    d_next.wait_recv()
    d_edge.wait_recv()
    yacc[0] += mm_t(scaled(d_rows(2), m0[2]), w_back(0))
    yacc[1] += mm_t(
        jnp.concatenate([scaled(d_rows(2), m1[2]), scaled(d_rows(3), m0[3])], axis=1),
        jnp.concatenate([w_back(1), w_back(0)], axis=1),
    )
    for f in range(2):
        ig_ref[0, f] = column_sum(yacc[f], True).astype(jnp.bfloat16).reshape(8, 32, 128)

    mine = (z - phase) // stride
    is_owner = ((z + stride - phase) % stride == 0) & (mine < owners)

    def piece_rows(j):
        return pl.ds(pl.multiple_of(p * chunk + j * piece, 16), piece)

    def zg_copy(j, w):
        return remote(
            full.at[core, piece_rows(j)], full.at[core, piece_rows(j)], zg_send.at[w], zg_recv.at[j], z_dev(w)
        )

    @pl.when(is_owner)
    def _():
        zbuf[pl.ds(z, 1)] = zs[pl.ds(pl.multiple_of(mine * piece, 16), piece), :][None]

        @pl.loop(1, z_n)
        def _(i):
            w = (z + i) % z_n
            remote(
                zs.at[pl.ds(0, piece)], zbuf.at[w], z_send.at[0], z_recv.at[w], z_dev(w)
            ).wait_recv()

        acc = zbuf[0].astype(jnp.float32)
        for w in range(1, z_n):
            acc += zbuf[w].astype(jnp.float32)
        full[core, piece_rows(mine)] = acc.astype(jnp.bfloat16)
        pl.loop(1, z_n)(lambda i: zg_copy(mine, (z + i) % z_n).start())

    @pl.loop(0, owners)
    def _(j):
        @pl.when(owner_of(j) != z)
        def _():
            zg_copy(j, owner_of(j)).wait_recv()

    def pg_copy(q, owner):
        return remote(
            full.at[core, chunk_rows(owner)], full.at[core, chunk_rows(owner)],
            pg_send.at[q], pg_recv.at[owner], plane_dev(q),
        )

    def cg_copy(q, side):
        return remote(
            full.at[side, chunk_rows(q)], full.at[side, chunk_rows(q)],
            cg_send.at[q], cg_recv.at[q], (dp, tm, other),
        )

    pl.loop(1, p_n)(lambda i: pg_copy((p + i) % p_n, p).start())
    cg_copy(p, core).start()

    @pl.loop(1, p_n)
    def _(i):
        q = (p + i) % p_n
        pg_copy(q, q).wait_recv()
        cg_copy(q, core).start()

    pl.loop(0, p_n)(lambda q: cg_copy(q, other).wait_recv())

    for copy in (x_next, x_edge, x_pair, x_fwd, d_pair, d_next, d_edge):
        copy.wait_send()

    @pl.loop(1, p_n)
    def _(i):
        q = (p + i) % p_n
        rs_copy(q).wait_send()
        pg_copy(q, p).wait_send()

    pl.loop(0, p_n)(lambda q: cg_copy(q, core).wait_send())

    @pl.loop(0, owners)
    def _(j):
        @pl.when(owner_of(j) != z)
        def _():
            z_copy(j).wait_send()

    @pl.when(is_owner)
    def _():
        pl.loop(1, z_n)(lambda i: zg_copy(mine, (z + i) % z_n).wait_send())


def on_device(dims, inputs, clip_lengths, weight, bias, cotangent):
    zh_n, tm_n = dims
    z_n, p_n = zh_n * Z_LO, tm_n // Z_LO
    chunk = ROWS // p_n
    tiles = chunk // 16
    piece = 16 * max(1, tiles // z_n)
    owners = chunk // piece
    block = inputs.shape
    dma = pltpu.SemaphoreType.DMA
    vmem, hbm, smem = (pl.BlockSpec(memory_space=m) for m in (pltpu.VMEM, pl.ANY, pltpu.SMEM))
    result, in_grad, full = pl.pallas_call(
        functools.partial(chip_kernel, dims),
        out_shape=(
            jax.ShapeDtypeStruct(block, jnp.bfloat16),
            jax.ShapeDtypeStruct(block, jnp.bfloat16),
            jax.ShapeDtypeStruct((2, ROWS, 128), jnp.bfloat16),
        ),
        in_specs=[smem, hbm, hbm, vmem, hbm],
        out_specs=(vmem, vmem, vmem),
        scratch_shapes=[
            pltpu.VMEM((4, 18, 32, 128), jnp.bfloat16),
            pltpu.VMEM((128, 512), jnp.float32),
            pltpu.VMEM((3, 3 * HALF, 1024), jnp.bfloat16),
            pltpu.VMEM((4, 18, 32, 128), jnp.bfloat16),
            pltpu.VMEM((3, 3, 3, 128, 128), jnp.bfloat16),
            pltpu.VMEM((2, 8, 32, 128), jnp.bfloat16),
            pltpu.VMEM((2, 256, 384), jnp.float32),
            pltpu.VMEM((ROWS, 128), jnp.bfloat16),
            pltpu.VMEM((p_n, chunk, 128), jnp.bfloat16),
            pltpu.VMEM((chunk, 128), jnp.bfloat16),
            pltpu.VMEM((z_n, piece, 128), jnp.bfloat16),
            dma((3,)), dma((4,)), dma((4,)), dma((3,)), dma((3,)),
            dma((p_n,)), dma((p_n,)), dma((owners,)), dma((z_n,)),
            dma((z_n,)), dma((owners,)), dma((p_n,)), dma((p_n,)), dma((p_n,)), dma((p_n,)),
        ],
        compiler_params=pltpu.CompilerParams(
            collective_id=0, has_side_effects=True, vmem_limit_bytes=40 * 1024 * 1024
        ),
        name="chip_kernel",
    )(clip_lengths, inputs, weight, bias.reshape(1, 128), cotangent)
    taps = full[:, :BIAS_ROW].reshape(2, 27, HALF, 128).transpose(1, 0, 2, 3)
    kern_grad = taps.astype(jnp.float32).reshape(3, 3, 3, 128, 128)
    bias_grad = jnp.sum(full[:, BIAS_ROW : BIAS_ROW + 16].astype(jnp.float32), axis=(0, 1))
    return result, in_grad, kern_grad, bias_grad


def solution(mesh):
    dims = (mesh.shape["dp"], mesh.shape["tm"])
    return jax.shard_map(
        functools.partial(on_device, dims),
        mesh=mesh,
        in_specs=(
            P("dp", "tm", "space", None, None),
            P("dp", None),
            P(),
            P(),
            P("dp", "tm", "space", None, None),
        ),
        out_specs=(
            P("dp", "tm", "space", None, None),
            P("dp", "tm", "space", None, None),
            P(),
            P(),
        ),
        check_vma=False,
    )
```

```python
import functools

import jax
import jax.numpy as jnp
from jax import lax
from jax.experimental import pallas as pl
from jax.experimental.pallas import tpu as pltpu
from jax.sharding import PartitionSpec as P

MESH = pl.DeviceIdType.MESH
Z_LO = 4
HALF = 64
ROWS = 28 * HALF
BIAS_ROW = 27 * HALF


def scalar_mask(ends, frame, lag):
    def clip(t):
        return sum((t >= end).astype(jnp.int32) for end in ends)

    earlier = frame - lag
    same = (clip(earlier) == clip(frame)) & (earlier >= 0)
    return same.astype(jnp.float32)


def scaled(values, mask):
    return values * jnp.full(values.shape, mask, jnp.float32).astype(values.dtype)


def column_sum(parts, back):
    count = parts.shape[0]
    col = lax.broadcasted_iota(jnp.int32, (count, 128), 0) % 32
    first, mid, last = parts[:, :128], parts[:, 128:256], parts[:, 256:]
    down, up = (last, first) if back else (first, last)
    down = jnp.where(col == 0, 0.0, pltpu.roll(down, 1, 0))
    up = jnp.where(col == 31, 0.0, pltpu.roll(up, count - 1, 0))
    return mid + down + up


def chip_kernel(
    dims, lens_hbm, x_hbm, w_hbm, bias_hbm, cot_hbm,
    out_ref, ig_ref, full,
    lens, bias, xs, xt, lt, dzs, wv, cotv, yacc, part, rsbuf, zs, zbuf,
    loc, xsend, xrecv, dsend, drecv, rs_send, rs_recv, z_send, z_recv,
    zg_send, zg_recv, pg_send, pg_recv, cg_send, cg_recv,
):
    zh_n, tm_n = dims
    z_n, p_n = zh_n * Z_LO, tm_n // Z_LO
    chunk, piece, owners = pieces(dims)

    dp, tm, core = lax.axis_index("dp"), lax.axis_index("tm"), lax.axis_index("space")
    other = 1 - core
    p, zl = tm // Z_LO, tm % Z_LO
    z = dp * Z_LO + zl
    after, before = (tm + 1) % tm_n, (tm + tm_n - 1) % tm_n

    def plane_dev(q):
        return (dp, q * Z_LO + zl, core)

    def z_dev(w):
        return (w // Z_LO, p * Z_LO + w % Z_LO, core)

    barrier = pltpu.get_barrier_semaphore()

    def greet(device):
        pl.semaphore_signal(barrier, inc=1, device_id=device, device_id_type=MESH)

    def remote(src, dst, send, recv, device):
        return pltpu.make_async_remote_copy(
            src_ref=src, dst_ref=dst, send_sem=send, recv_sem=recv, device_id=device, device_id_type=MESH
        )

    own = pl.ds(1 + 8 * core, 8)
    edge_row = 7 * other
    edge = pl.ds(1 + 8 * core + edge_row, 1)
    inner = pl.ds(1 + 9 * core, 7)
    two, later = pl.ds(0, 2), pl.ds(2, 2)

    greet((dp, tm, other))
    for near in (before, after):
        greet((dp, near, core))
        greet((dp, near, other))
    pl.loop(1, p_n)(lambda i: greet(plane_dev((p + i) % p_n)))
    pl.loop(1, z_n)(lambda i: greet(z_dev((z + i) % z_n)))

    get_x = pltpu.make_async_copy(x_hbm.at[0], xs.at[later, own], loc.at[0])
    get_w = pltpu.make_async_copy(w_hbm, wv, loc.at[1])
    get_cot = pltpu.make_async_copy(cot_hbm.at[0], cotv, loc.at[2])
    get_lens = pltpu.make_async_copy(lens_hbm, lens, loc.at[3])
    get_bias = pltpu.make_async_copy(bias_hbm, bias, loc.at[4])
    for copy in (get_x, get_w, get_lens, get_cot, get_bias):
        copy.start()
    for f in range(4):
        for r in (0, 17):
            xs[f, r] = jnp.zeros((32, 128), jnp.bfloat16)
            dzs[f, r] = jnp.zeros((32, 128), jnp.bfloat16)

    @pl.when(tm == 0)
    def _():
        xs[two, pl.ds(1, 16)] = jnp.zeros((2, 16, 32, 128), jnp.bfloat16)

    @pl.when(tm == tm_n - 1)
    def _():
        dzs[later, pl.ds(1, 16)] = jnp.zeros((2, 16, 32, 128), jnp.bfloat16)

    get_lens.wait()
    ends = [lens[0, 0]]
    for j in range(1, lens.shape[1]):
        ends.append(ends[-1] + lens[0, j])
    base = 2 * tm
    m0 = [scalar_mask(ends, base + t, 2) for t in range(4)]
    m1 = [scalar_mask(ends, base + t, 1) for t in range(3)]

    pl.semaphore_wait(barrier, 5 + p_n - 1 + z_n - 1)

    x_next = remote(x_hbm.at[0], xs.at[two, own], xsend.at[1], xrecv.at[1], (dp, after, core))
    x_edge = remote(
        x_hbm.at[0, two, pl.ds(edge_row, 1)], xs.at[two, edge], xsend.at[2], xrecv.at[2], (dp, after, other)
    )
    x_pair = remote(x_hbm.at[0], xs.at[later, own], xsend.at[0], xrecv.at[0], (dp, tm, other))
    x_fwd = remote(xs.at[two, inner], xs.at[two, inner], xsend.at[3], xrecv.at[3], (dp, tm, other))

    @pl.when(tm < tm_n - 1)
    def _():
        x_next.start()
        x_edge.start()

    x_pair.start()

    def x_rows(f):
        return jnp.concatenate(
            [xs[f, pl.ds(8 * core + a, 8)].reshape(256, 128) for a in range(3)], axis=1
        )

    def w_fwd(k):
        return jnp.concatenate(
            [jnp.concatenate([wv[k, a, b] for b in range(3)], axis=1) for a in range(3)], axis=0
        )

    def mm(lhs, rhs):
        return jnp.dot(lhs, rhs, preferred_element_type=jnp.float32)

    def turned(f):
        xt[...] = xs[f, pl.ds(1, 16)].reshape(512, 128).astype(jnp.float32).T
        mid = xt[pl.ds(pl.multiple_of(HALF * core, HALF), HALF), :]
        col = lax.broadcasted_iota(jnp.int32, (HALF, 512), 1) % 32
        left = jnp.where(col == 0, 0.0, pltpu.roll(mid, 1, 1))
        right = jnp.where(col == 31, 0.0, pltpu.roll(mid, 511, 1))
        block = jnp.concatenate([left, mid, right], axis=0)
        for t in range(2):
            k = f - t
            if k < 0 or k > 2:
                continue
            kept = block if k == 2 else block * (m1[t] if k == 1 else m0[t])
            lt[k, :, pl.ds(512 * t, 512)] = kept.astype(jnp.bfloat16)

    get_x.wait()
    get_w.wait()
    x_pair.wait_recv()
    yacc[0] = mm(x_rows(2), w_fwd(2))
    yacc[1] = mm(
        jnp.concatenate([x_rows(3), scaled(x_rows(2), m1[1])], axis=1),
        jnp.concatenate([w_fwd(2), w_fwd(1)], axis=0),
    )
    turned(2)
    turned(3)
    get_cot.wait()
    get_bias.wait()

    @pl.when(tm > 0)
    def _():
        x_next.wait_recv()
        x_fwd.start()
        x_edge.wait_recv()

    yacc[0] += mm(
        jnp.concatenate([scaled(x_rows(1), m1[0]), scaled(x_rows(0), m0[0])], axis=1),
        jnp.concatenate([w_fwd(1), w_fwd(0)], axis=0),
    )
    yacc[1] += mm(scaled(x_rows(1), m0[1]), w_fwd(0))

    bias_part = jnp.zeros((16, 128), jnp.float32)
    for f in range(2):
        zed = column_sum(yacc[f], False) + bias[...]
        sig = jax.nn.sigmoid(zed)
        out_ref[0, f] = (zed * sig).astype(jnp.bfloat16).reshape(8, 32, 128)
        cot = cotv[f].reshape(256, 128).astype(jnp.float32)
        dz = (cot * sig * (1.0 + zed * (1.0 - sig))).astype(jnp.bfloat16)
        dzs[f, own] = dz.reshape(8, 32, 128)
        bias_part += jnp.sum(dz.astype(jnp.float32).reshape(16, 16, 128), axis=0)

    d_pair = remote(dzs.at[two, own], dzs.at[two, own], dsend.at[0], drecv.at[0], (dp, tm, other))
    d_next = remote(dzs.at[two, own], dzs.at[later, own], dsend.at[1], drecv.at[1], (dp, before, core))
    d_edge = remote(dzs.at[two, edge], dzs.at[later, edge], dsend.at[2], drecv.at[2], (dp, before, other))
    d_pair.start()

    @pl.when(zl > 0)
    def _():
        d_next.start()
        d_edge.start()

    part[pl.ds(BIAS_ROW, 16), :] = bias_part.astype(jnp.bfloat16)
    part[pl.ds(BIAS_ROW + 16, ROWS - BIAS_ROW - 16), :] = jnp.zeros((ROWS - BIAS_ROW - 16, 128), jnp.bfloat16)
    pl.when(tm > 0)(x_fwd.wait_recv)
    turned(0)
    turned(1)
    d_pair.wait_recv()

    right_side = jnp.concatenate(
        [
            jnp.concatenate([dzs[t, pl.ds(2 - a, 16)].reshape(512, 128) for a in range(3)], axis=1)
            for t in range(2)
        ],
        axis=0,
    )

    def chunk_rows(q):
        return pl.ds(pl.multiple_of(q * chunk, 16), chunk)

    def rs_start(q):
        @pl.when(q != p)
        def _():
            slot = (p + p_n - q - 1) % p_n
            remote(part.at[chunk_rows(q)], rsbuf.at[slot], rs_send, rs_recv, plane_dev(q)).start()

    sent = 0
    for k in range(3):
        grad = mm(lt[k], right_side)
        for a in range(3):
            for b in range(3):
                tap = (k * 3 + a) * 3 + b
                part[pl.ds(tap * HALF, HALF), :] = grad[
                    b * HALF : (b + 1) * HALF, a * 128 : (a + 1) * 128
                ].astype(jnp.bfloat16)
        ready = p_n if k == 2 else (k + 1) * 9 * HALF // chunk
        pl.loop(sent, ready)(rs_start)
        sent = ready

    def d_rows(f):
        return jnp.concatenate(
            [dzs[f, pl.ds(8 * core + 2 - a, 8)].reshape(256, 128) for a in range(3)], axis=1
        )

    def w_back(k):
        return jnp.concatenate([wv[k, a].reshape(384, 128) for a in range(3)], axis=1)

    def mm_t(lhs, rhs):
        return lax.dot_general(lhs, rhs, (((1,), (1,)), ((), ())), preferred_element_type=jnp.float32)

    yacc[0] = mm_t(
        jnp.concatenate([d_rows(0), scaled(d_rows(1), m1[1])], axis=1),
        jnp.concatenate([w_back(2), w_back(1)], axis=1),
    )
    yacc[1] = mm_t(d_rows(1), w_back(2))

    remote(rsbuf, rsbuf, rs_send, rs_recv, plane_dev(p)).wait_recv()
    total = part[chunk_rows(p), :].astype(jnp.float32)
    for q in range(p_n - 1):
        total += rsbuf[q].astype(jnp.float32)
    zs[...] = total.astype(jnp.bfloat16)

    def owner_of(j):
        return (z_n + j - owners // 2) % z_n

    mine = (z + owners // 2) % z_n
    is_owner = mine < owners

    def zs_rows(j):
        return pl.ds(pl.multiple_of(j * piece, 16), piece)

    @pl.loop(0, owners)
    def _(j):
        w = owner_of(j)

        @pl.when(w != z)
        def _():
            slot = (z + z_n - w - 1) % z_n
            remote(zs.at[zs_rows(j)], zbuf.at[slot], z_send, z_recv, z_dev(w)).start()

    @pl.when(zl == 0)
    def _():
        @pl.when(tm > 0)
        def _():
            d_next.start()
            d_edge.start()

    def piece_rows(owner, j):
        return pl.ds(pl.multiple_of(owner * chunk + j * piece, 16), piece)

    def zg_copy(j, w):
        return remote(
            full.at[core, piece_rows(p, j)], full.at[core, piece_rows(p, j)], zg_send, zg_recv.at[j], z_dev(w)
        )

    def pg_start(j):
        rows = piece_rows(p, j)

        @pl.loop(1, p_n)
        def _(i):
            remote(
                full.at[core, rows], full.at[core, rows], pg_send, pg_recv.at[p], plane_dev((p + i) % p_n)
            ).start()

    @pl.when(is_owner)
    def _():
        remote(zbuf, zbuf, z_send, z_recv, z_dev(z)).wait_recv()
        acc = zs[zs_rows(mine), :].astype(jnp.float32)
        for w in range(z_n - 1):
            acc += zbuf[w].astype(jnp.float32)
        full[core, piece_rows(p, mine)] = acc.astype(jnp.bfloat16)

        @pl.loop(0, z_n)
        def _(w):
            pl.when(w != z)(lambda: zg_copy(mine, w).start())

        pg_start(mine)

    for j in sorted(range(owners), key=lambda j: abs(j - owners // 2)):
        @pl.when(owner_of(j) != z)
        def _():
            zg_copy(j, owner_of(j)).wait_recv()
            pg_start(j)

    def cg_copy(rows):
        return remote(full.at[core, rows], full.at[core, rows], cg_send, cg_recv, (dp, tm, other))

    cg_copy(chunk_rows(p)).start()

    @pl.when(tm < tm_n - 1)
    def _():
        d_next.wait_recv()
        d_edge.wait_recv()

    yacc[0] += mm_t(scaled(d_rows(2), m0[2]), w_back(0))
    yacc[1] += mm_t(
        jnp.concatenate([scaled(d_rows(2), m1[2]), scaled(d_rows(3), m0[3])], axis=1),
        jnp.concatenate([w_back(1), w_back(0)], axis=1),
    )
    for f in range(2):
        ig_ref[0, f] = column_sum(yacc[f], True).astype(jnp.bfloat16).reshape(8, 32, 128)

    @pl.loop(1, p_n)
    def _(i):
        q = (p + i) % p_n
        rows = chunk_rows(q)
        remote(full.at[core, rows], full.at[core, rows], pg_send, pg_recv.at[q], plane_dev(q)).wait_recv()
        cg_copy(rows).start()

    @pl.when(tm < tm_n - 1)
    def _():
        x_next.wait_send()
        x_edge.wait_send()

    x_pair.wait_send()
    d_pair.wait_send()

    @pl.when(tm > 0)
    def _():
        x_fwd.wait_send()
        d_next.wait_send()
        d_edge.wait_send()

    rest = pl.ds(0, (p_n - 1) * chunk)
    remote(part.at[rest], part.at[rest], rs_send, rs_recv, plane_dev(p)).wait_send()

    @pl.when(is_owner)
    def _():
        most = zs.at[pl.ds(0, (owners - 1) * piece)]
        remote(most, most, z_send, z_recv, z_dev(z)).wait_send()
        remote(zbuf, zbuf, zg_send, z_recv, z_dev(z)).wait_send()

    @pl.when(jnp.logical_not(is_owner))
    def _():
        remote(zs, zs, z_send, z_recv, z_dev(z)).wait_send()

    remote(full.at[core, rest], full.at[core, rest], pg_send, pg_recv.at[p], plane_dev(p)).wait_send()
    everything = remote(full.at[core], full.at[other], cg_send, cg_recv, (dp, tm, other))
    everything.wait_send()
    everything.wait_recv()


def finish_kernel(out_in, ig_in, full, out_ref, ig_ref, grad_ref, bias_ref, buf, bias_buf, sems):
    copies = [
        pltpu.make_async_copy(out_in, out_ref, sems.at[0]),
        pltpu.make_async_copy(ig_in, ig_ref, sems.at[1]),
    ]
    for k in range(3):
        for a in range(3):
            for b in range(3):
                tap = (k * 3 + a) * 3 + b
                for side in range(2):
                    buf[k, a, b, pl.ds(side * HALF, HALF), :] = full[side, pl.ds(tap * HALF, HALF), :].astype(
                        jnp.float32
                    )
            copies.append(pltpu.make_async_copy(buf.at[k, a], grad_ref.at[k, a], sems.at[3 + 3 * k + a]))
            copies[-1].start()
    copies[0].start()
    copies[1].start()
    terms = full[:, pl.ds(BIAS_ROW, 16), :].astype(jnp.float32)
    bias_buf[...] = jnp.sum(terms[0] + terms[1], axis=0, keepdims=True)
    copies.append(pltpu.make_async_copy(bias_buf, bias_ref, sems.at[2]))
    copies[-1].start()
    for copy in copies:
        copy.wait()


def pieces(dims):
    zh_n, tm_n = dims
    z_n, p_n = zh_n * Z_LO, tm_n // Z_LO
    chunk = ROWS // p_n
    piece = 16 * max(1, chunk // 16 // z_n)
    return chunk, piece, chunk // piece


def on_device(dims, inputs, clip_lengths, weight, bias, cotangent):
    zh_n, tm_n = dims
    z_n, p_n = zh_n * Z_LO, tm_n // Z_LO
    chunk, piece, owners = pieces(dims)
    block = inputs.shape
    dma = pltpu.SemaphoreType.DMA
    vmem, hbm = (pl.BlockSpec(memory_space=m) for m in (pltpu.VMEM, pltpu.HBM))
    operands = (clip_lengths, inputs, weight, bias.reshape(1, 128), cotangent)
    result, in_grad, full = pl.pallas_call(
        functools.partial(chip_kernel, dims),
        out_shape=(
            jax.ShapeDtypeStruct(block, jnp.bfloat16),
            jax.ShapeDtypeStruct(block, jnp.bfloat16),
            jax.ShapeDtypeStruct((2, ROWS, 128), jnp.bfloat16),
        ),
        in_specs=[hbm, hbm, hbm, hbm, hbm],
        out_specs=(vmem, vmem, vmem),
        scratch_shapes=[
            pltpu.SMEM(clip_lengths.shape, jnp.int32),
            pltpu.VMEM((1, 128), jnp.float32),
            pltpu.VMEM((4, 18, 32, 128), jnp.bfloat16),
            pltpu.VMEM((128, 512), jnp.float32),
            pltpu.VMEM((3, 3 * HALF, 1024), jnp.bfloat16),
            pltpu.VMEM((4, 18, 32, 128), jnp.bfloat16),
            pltpu.VMEM((3, 3, 3, 128, 128), jnp.bfloat16),
            pltpu.VMEM((2, 8, 32, 128), jnp.bfloat16),
            pltpu.VMEM((2, 256, 384), jnp.float32),
            pltpu.VMEM((ROWS, 128), jnp.bfloat16),
            pltpu.VMEM((p_n - 1, chunk, 128), jnp.bfloat16),
            pltpu.VMEM((chunk, 128), jnp.bfloat16),
            pltpu.VMEM((z_n - 1, piece, 128), jnp.bfloat16),
            dma((5,)), dma((4,)), dma((4,)), dma((3,)), dma((3,)),
            dma, dma, dma, dma, dma, dma((owners,)), dma, dma((p_n,)), dma, dma,
        ],
        compiler_params=pltpu.CompilerParams(
            collective_id=0, has_side_effects=True, vmem_limit_bytes=40 * 1024 * 1024
        ),
        name="chip_kernel",
    )(*(pltpu.with_memory_space_constraint(a, pltpu.HBM) for a in operands))
    result, in_grad, kern_grad, bias_grad = pl.pallas_call(
        finish_kernel,
        out_shape=(
            jax.ShapeDtypeStruct(block, jnp.bfloat16),
            jax.ShapeDtypeStruct(block, jnp.bfloat16),
            jax.ShapeDtypeStruct((3, 3, 3, 128, 128), jnp.float32),
            jax.ShapeDtypeStruct((1, 128), jnp.float32),
        ),
        in_specs=[vmem, vmem, vmem],
        out_specs=(hbm, hbm, hbm, hbm),
        scratch_shapes=[
            pltpu.VMEM((3, 3, 3, 128, 128), jnp.float32),
            pltpu.VMEM((1, 128), jnp.float32),
            dma((12,)),
        ],
        compiler_params=pltpu.CompilerParams(vmem_limit_bytes=32 * 1024 * 1024),
        name="finish_kernel",
    )(result, in_grad, full)
    return result, in_grad, kern_grad, bias_grad.reshape(128)


def solution(mesh):
    dims = (mesh.shape["dp"], mesh.shape["tm"])
    return jax.shard_map(
        functools.partial(on_device, dims),
        mesh=mesh,
        in_specs=(
            P("dp", "tm", "space", None, None),
            P("dp", None),
            P(),
            P(),
            P("dp", "tm", "space", None, None),
        ),
        out_specs=(
            P("dp", "tm", "space", None, None),
            P("dp", "tm", "space", None, None),
            P(),
            P(),
        ),
        check_vma=False,
    )
```

```python
import functools

import jax
import jax.numpy as jnp
from jax import lax
from jax.experimental import pallas as pl
from jax.experimental.pallas import tpu as pltpu
from jax.sharding import PartitionSpec as P

MESH = pl.DeviceIdType.MESH
Z_LO = 4
PLANE_Y = 4
HALF = 64
ROWS = 28 * HALF
TILES = 9 * HALF // 16


def tile_row(p_n, k, tile):
    chunk, per = ROWS // p_n, TILES // p_n
    if k < 3 and tile < per * p_n:
        return tile // per * chunk + (k * per + tile % per) * 16
    extra = k * (TILES - per * p_n) + (tile - per * p_n if k < 3 else tile)
    return extra % p_n * chunk + (3 * per + extra // p_n) * 16


def scalar_mask(ends, frame, lag):
    def clip(t):
        return sum((t >= end).astype(jnp.int32) for end in ends)

    earlier = frame - lag
    same = (clip(earlier) == clip(frame)) & (earlier >= 0)
    return same.astype(jnp.float32)


def scaled(values, mask):
    return values * jnp.full(values.shape, mask, jnp.float32).astype(values.dtype)


def column_sum(parts, back):
    count = parts.shape[0]
    col = lax.broadcasted_iota(jnp.int32, (count, 128), 0) % 32
    first, mid, last = parts[:, :128], parts[:, 128:256], parts[:, 256:]
    down, up = (last, first) if back else (first, last)
    down = jnp.where(col == 0, 0.0, pltpu.roll(down, 1, 0))
    up = jnp.where(col == 31, 0.0, pltpu.roll(up, count - 1, 0))
    return mid + down + up


def chip_kernel(
    dims, lens_hbm, x_hbm, w_hbm, bias_hbm, cot_hbm,
    out_ref, ig_ref, full,
    lens, bias, xs, xt, lt, dzs, wv, cotv, yacc, part, rsbuf, zs, zbuf,
    known, loc, xsend, xrecv, dsend, drecv, rs_send, rs_recv, z_send, z_recv,
    zg_send, zg_recv, pg_send, pg_recv, cg_send, cg_recv,
):
    zh_n, tm_n = dims
    z_n, p_n = zh_n * Z_LO, tm_n // Z_LO
    chunk, piece, owners = pieces(dims)
    rounds = rounds_of(z_n)

    dp, tm, core = lax.axis_index("dp"), lax.axis_index("tm"), lax.axis_index("space")
    other = 1 - core
    p, zl = tm // Z_LO, tm % Z_LO
    z = dp * Z_LO + zl
    after, before = (tm + 1) % tm_n, (tm + tm_n - 1) % tm_n

    def plane_dev(q):
        return (dp, q * Z_LO + zl, core)

    def z_dev(w):
        return (w // Z_LO, p * Z_LO + w % Z_LO, core)

    barrier = pltpu.get_barrier_semaphore()

    def greet(device):
        pl.semaphore_signal(barrier, inc=1, device_id=device, device_id_type=MESH)

    def remote(src, dst, send, recv, device):
        return pltpu.make_async_remote_copy(
            src_ref=src, dst_ref=dst, send_sem=send, recv_sem=recv, device_id=device, device_id_type=MESH
        )

    own = pl.ds(1 + 8 * core, 8)
    edge_row = 7 * other
    edge = pl.ds(1 + 8 * core + edge_row, 1)
    inner = pl.ds(1 + 9 * core, 7)
    two, later = pl.ds(0, 2), pl.ds(2, 2)

    greet((dp, tm, other))
    for there, near in ((tm > 0, before), (tm < tm_n - 1, after)):
        @pl.when(there)
        def _():
            greet((dp, near, core))
            greet((dp, near, other))

    pl.loop(1, p_n)(lambda i: greet(plane_dev((p + i) % p_n)))
    greet(z_dev((z + 1) % z_n))
    greet(z_dev((z + z_n - 1) % z_n))

    get_x = pltpu.make_async_copy(x_hbm.at[0], xs.at[later, own], loc.at[0])
    get_w = pltpu.make_async_copy(w_hbm, wv, loc.at[1])
    get_cot = pltpu.make_async_copy(cot_hbm.at[0], cotv, loc.at[2])
    get_lens = pltpu.make_async_copy(lens_hbm, lens, loc.at[3])
    get_bias = pltpu.make_async_copy(bias_hbm, bias, loc.at[4])
    for copy in (get_x, get_w, get_lens, get_cot, get_bias):
        copy.start()
    for f in range(4):
        for r in (0, 17):
            xs[f, r] = jnp.zeros((32, 128), jnp.bfloat16)
            dzs[f, r] = jnp.zeros((32, 128), jnp.bfloat16)

    @pl.when(tm == 0)
    def _():
        xs[two, pl.ds(1, 16)] = jnp.zeros((2, 16, 32, 128), jnp.bfloat16)

    @pl.when(tm == tm_n - 1)
    def _():
        dzs[later, pl.ds(1, 16)] = jnp.zeros((2, 16, 32, 128), jnp.bfloat16)

    get_lens.wait()
    ends = [lens[0, 0]]
    for j in range(1, lens.shape[1]):
        ends.append(ends[-1] + lens[0, j])
    base = 2 * tm
    m0 = [scalar_mask(ends, base + t, 2) for t in range(4)]
    m1 = [scalar_mask(ends, base + t, 1) for t in range(3)]

    get_x.wait()
    sides = (tm + tm_n - 1) // tm_n + (2 * (tm_n - 1) - tm) // tm_n
    pl.semaphore_wait(barrier, 1 + (p_n - 1) + 2 + 2 * sides)

    def tell(r):
        for w in (z + rounds[r], z + z_n - rounds[r]):
            pl.semaphore_signal(known.at[r], inc=1, device_id=z_dev(w % z_n), device_id_type=MESH)

    def hear(r):
        pl.semaphore_wait(known.at[r], 2)

    tell(0)

    x_next = [
        remote(xs.at[2 + f, own], xs.at[f, own], xsend.at[1 + 4 * f], xrecv.at[1 + 4 * f], (dp, after, core))
        for f in range(2)
    ]
    x_edge = remote(
        xs.at[later, edge], xs.at[two, edge], xsend.at[2], xrecv.at[2], (dp, after, other)
    )
    x_pair = remote(xs.at[later, own], xs.at[later, own], xsend.at[0], xrecv.at[0], (dp, tm, other))
    x_fwd = [
        remote(xs.at[f, inner], xs.at[f, inner], xsend.at[3 + f], xrecv.at[3 + f], (dp, tm, other))
        for f in range(2)
    ]

    @pl.when(tm < tm_n - 1)
    def _():
        x_edge.start()
        x_next[1].start()
        x_next[0].start()

    x_pair.start()

    def x_rows(f):
        return jnp.concatenate(
            [xs[f, pl.ds(8 * core + a, 8)].reshape(256, 128) for a in range(3)], axis=1
        )

    def w_fwd(k):
        return jnp.concatenate(
            [jnp.concatenate([wv[k, a, b] for b in range(3)], axis=1) for a in range(3)], axis=0
        )

    def mm(lhs, rhs):
        return jnp.dot(lhs, rhs, preferred_element_type=jnp.float32)

    def turned(f):
        xt[...] = xs[f, pl.ds(1, 16)].reshape(512, 128).astype(jnp.float32).T
        mid = xt[pl.ds(pl.multiple_of(HALF * core, HALF), HALF), :]
        col = lax.broadcasted_iota(jnp.int32, (HALF, 512), 1) % 32
        left = jnp.where(col == 0, 0.0, pltpu.roll(mid, 1, 1))
        right = jnp.where(col == 31, 0.0, pltpu.roll(mid, 511, 1))
        block = jnp.concatenate([left, mid, right], axis=0)
        for t in range(2):
            k = f - t
            if k < 0 or k > 2:
                continue
            kept = block if k == 2 else block * (m1[t] if k == 1 else m0[t])
            lt[k, :, pl.ds(512 * t, 512)] = kept.astype(jnp.bfloat16)

    get_w.wait()
    x_pair.wait_recv()
    yacc[0] = mm(x_rows(2), w_fwd(2))
    yacc[1] = mm(
        jnp.concatenate([x_rows(3), scaled(x_rows(2), m1[1])], axis=1),
        jnp.concatenate([w_fwd(2), w_fwd(1)], axis=0),
    )
    turned(2)
    turned(3)
    get_cot.wait()
    get_bias.wait()

    def halo_frame(f):
        @pl.when(tm > 0)
        def _():
            x_next[f].wait_recv()
            x_fwd[f].start()

    def finish_frame(f):
        zed = column_sum(yacc[f], False) + bias[...]
        sig = jax.nn.sigmoid(zed)
        out_ref[0, f] = (zed * sig).astype(jnp.bfloat16).reshape(8, 32, 128)
        cot = cotv[f].reshape(256, 128).astype(jnp.float32)
        dz = (cot * sig * (1.0 + zed * (1.0 - sig))).astype(jnp.bfloat16)
        dzs[f, own] = dz.reshape(8, 32, 128)
        d_pair[f].start()
        return jnp.sum(dz.astype(jnp.float32).reshape(16, 16, 128), axis=0)

    d_pair = [
        remote(dzs.at[f, own], dzs.at[f, own], dsend.at[3 * f], drecv.at[3 * f], (dp, tm, other))
        for f in range(2)
    ]

    pl.when(tm > 0)(x_edge.wait_recv)
    halo_frame(1)
    yacc[0] += mm(scaled(x_rows(1), m1[0]), w_fwd(1))
    yacc[1] += mm(scaled(x_rows(1), m0[1]), w_fwd(0))
    bias_part = finish_frame(1)
    halo_frame(0)
    yacc[0] += mm(scaled(x_rows(0), m0[0]), w_fwd(0))
    bias_part += finish_frame(0)

    d_next = remote(dzs.at[two, own], dzs.at[later, own], dsend.at[1], drecv.at[1], (dp, before, core))
    d_edge = remote(dzs.at[two, edge], dzs.at[later, edge], dsend.at[2], drecv.at[2], (dp, before, other))

    early = dp < zh_n // 2
    near = zl > 0

    def d_start():
        d_next.start()
        d_edge.start()

    pl.when(near | (early & (tm > 0)))(d_start)

    part[pl.ds(tile_row(p_n, 3, 0), 16), :] = bias_part.astype(jnp.bfloat16)
    for spare in range(1, ROWS // 16 - 3 * TILES):
        part[pl.ds(tile_row(p_n, 3, spare), 16), :] = jnp.zeros((16, 128), jnp.bfloat16)
    for f in (1, 0):
        pl.when(tm > 0)(x_fwd[f].wait_recv)
        turned(f)
    d_pair[1].wait_recv()
    d_pair[0].wait_recv()

    right_side = jnp.concatenate(
        [
            jnp.concatenate([dzs[t, pl.ds(2 - a, 16)].reshape(512, 128) for a in range(3)], axis=1)
            for t in range(2)
        ],
        axis=0,
    )

    def chunk_rows(q):
        return pl.ds(pl.multiple_of(q * chunk, 16), chunk)

    x_n = p_n // PLANE_Y
    xq = [(p // PLANE_Y + dx) % x_n * PLANE_Y for dx in range(x_n)]
    yq = [(p % PLANE_Y + dy) % PLANE_Y for dy in range(PLANE_Y)]
    far_first = sorted(range(x_n), key=lambda dx: -min(dx, x_n - dx))

    per = TILES // p_n * 16
    for k in range(3):
        grad = mm(lt[k], right_side)
        for a in range(3):
            for b in range(3):
                for j in range(HALF // 16):
                    block = grad[b * HALF + j * 16 : b * HALF + j * 16 + 16, a * 128 : (a + 1) * 128]
                    row = tile_row(p_n, k, (a * 3 + b) * (HALF // 16) + j)
                    part[pl.ds(row, 16), :] = block.astype(jnp.bfloat16)
        count = per if k < 2 else chunk - 2 * per

        for dx in far_first:
            for dy in range(0 if dx else 1, PLANE_Y):
                q = xq[dx] + yq[dy]
                remote(
                    part.at[pl.ds(pl.multiple_of(q * chunk + k * per, 16), count)],
                    rsbuf.at[dx * PLANE_Y + dy - 1, pl.ds(k * per, count)], rs_send, rs_recv, plane_dev(q),
                ).start()

    hear(0)
    if len(rounds) > 1:
        tell(1)

    def d_rows(f):
        return jnp.concatenate(
            [dzs[f, pl.ds(8 * core + 2 - a, 8)].reshape(256, 128) for a in range(3)], axis=1
        )

    def w_back(k):
        return jnp.concatenate([wv[k, a].reshape(384, 128) for a in range(3)], axis=1)

    def mm_t(lhs, rhs):
        return lax.dot_general(lhs, rhs, (((1,), (1,)), ((), ())), preferred_element_type=jnp.float32)

    yacc[0] = mm_t(
        jnp.concatenate([d_rows(0), scaled(d_rows(1), m1[1])], axis=1),
        jnp.concatenate([w_back(2), w_back(1)], axis=1),
    )
    yacc[1] = mm_t(d_rows(1), w_back(2))

    for r in range(1, len(rounds) - 1):
        hear(r)
        tell(r + 1)

    remote(rsbuf, rsbuf, rs_send, rs_recv, plane_dev(p)).wait_recv()
    total = part[chunk_rows(p), :].astype(jnp.float32)
    for q in range(p_n - 1):
        total += rsbuf[q].astype(jnp.float32)
    zs[...] = total.astype(jnp.bfloat16)

    def owner_of(j):
        return (z_n + j - (owners - 2)) % z_n

    mine = (z + owners - 2) % z_n
    is_owner = mine < owners

    def zs_rows(j):
        return pl.ds(pl.multiple_of(j * piece, 16), piece)

    if len(rounds) > 1:
        hear(len(rounds) - 1)

    @pl.loop(0, owners)
    def _(i):
        j = owners - 1 - i
        w = owner_of(j)

        @pl.when(w != z)
        def _():
            slot = (z + z_n - w - 1) % z_n
            remote(zs.at[zs_rows(j)], zbuf.at[slot], z_send, z_recv, z_dev(w)).start()

    def piece_rows(owner, j):
        return pl.ds(pl.multiple_of(owner * chunk + j * piece, 16), piece)

    def zg_copy(j, w):
        return remote(
            full.at[core, piece_rows(p, j)], full.at[core, piece_rows(p, j)], zg_send, zg_recv.at[j], z_dev(w)
        )

    def pg_start(j):
        rows = piece_rows(p, j)

        for dx in far_first:
            @pl.loop(0 if dx else 1, PLANE_Y)
            def _(dy):
                q = xq[dx] + (p % PLANE_Y + dy) % PLANE_Y
                remote(full.at[core, rows], full.at[core, rows], pg_send, pg_recv.at[p], plane_dev(q)).start()

    @pl.when(is_owner)
    def _():
        remote(zbuf, zbuf, z_send, z_recv, z_dev(z)).wait_recv()
        acc = zs[zs_rows(mine), :].astype(jnp.float32)
        for w in range(z_n - 1):
            acc += zbuf[w].astype(jnp.float32)
        full[core, piece_rows(p, mine)] = acc.astype(jnp.bfloat16)

        @pl.loop(0, z_n)
        def _(w):
            pl.when(w != z)(lambda: zg_copy(mine, w).start())

        pg_start(mine)

    for j in sorted(range(owners), key=lambda j: abs(j - (owners - 2))):
        @pl.when(owner_of(j) != z)
        def _():
            zg_copy(j, owner_of(j)).wait_recv()
            pg_start(j)

    pl.when(jnp.logical_not(near | early) & (tm > 0))(d_start)

    def cg_copy(rows):
        return remote(full.at[core, rows], full.at[core, rows], cg_send, cg_recv, (dp, tm, other))

    cg_copy(chunk_rows(p)).start()

    def rest_of_in_grad():
        @pl.when(tm < tm_n - 1)
        def _():
            d_next.wait_recv()
            d_edge.wait_recv()

        yacc[0] += mm_t(scaled(d_rows(2), m0[2]), w_back(0))
        yacc[1] += mm_t(
            jnp.concatenate([scaled(d_rows(2), m1[2]), scaled(d_rows(3), m0[3])], axis=1),
            jnp.concatenate([w_back(1), w_back(0)], axis=1),
        )
        for f in range(2):
            ig_ref[0, f] = column_sum(yacc[f], True).astype(jnp.bfloat16).reshape(8, 32, 128)

    pl.when(early)(rest_of_in_grad)

    @pl.loop(1, p_n)
    def _(i):
        q = (p + i) % p_n
        rows = chunk_rows(q)
        remote(full.at[core, rows], full.at[core, rows], pg_send, pg_recv.at[q], plane_dev(q)).wait_recv()
        cg_copy(rows).start()

    pl.when(jnp.logical_not(early))(rest_of_in_grad)

    @pl.when(tm < tm_n - 1)
    def _():
        x_next[0].wait_send()
        x_next[1].wait_send()
        x_edge.wait_send()

    x_pair.wait_send()
    d_pair[0].wait_send()
    d_pair[1].wait_send()

    @pl.when(tm > 0)
    def _():
        x_fwd[0].wait_send()
        x_fwd[1].wait_send()
        d_next.wait_send()
        d_edge.wait_send()

    rest = pl.ds(0, (p_n - 1) * chunk)
    remote(part.at[rest], part.at[rest], rs_send, rs_recv, plane_dev(p)).wait_send()

    @pl.when(is_owner)
    def _():
        most = zs.at[pl.ds(0, (owners - 1) * piece)]
        remote(most, most, z_send, z_recv, z_dev(z)).wait_send()
        remote(zbuf, zbuf, zg_send, z_recv, z_dev(z)).wait_send()

    @pl.when(jnp.logical_not(is_owner))
    def _():
        remote(zs, zs, z_send, z_recv, z_dev(z)).wait_send()

    remote(full.at[core, rest], full.at[core, rest], pg_send, pg_recv.at[p], plane_dev(p)).wait_send()
    everything = remote(full.at[core], full.at[other], cg_send, cg_recv, (dp, tm, other))
    everything.wait_send()
    everything.wait_recv()


def finish_kernel(p_n, out_in, ig_in, full, out_ref, ig_ref, grad_ref, bias_ref, buf, bias_buf, sems):
    copies = [
        pltpu.make_async_copy(out_in, out_ref, sems.at[0]),
        pltpu.make_async_copy(ig_in, ig_ref, sems.at[1]),
    ]
    for k in range(3):
        for a in range(3):
            for b in range(3):
                for side in range(2):
                    for j in range(HALF // 16):
                        row = tile_row(p_n, k, (a * 3 + b) * (HALF // 16) + j)
                        buf[k, a, b, pl.ds(side * HALF + j * 16, 16), :] = full[
                            side, pl.ds(row, 16), :
                        ].astype(jnp.float32)
            copies.append(pltpu.make_async_copy(buf.at[k, a], grad_ref.at[k, a], sems.at[3 + 3 * k + a]))
            copies[-1].start()
    copies[0].start()
    copies[1].start()
    terms = full[:, pl.ds(tile_row(p_n, 3, 0), 16), :].astype(jnp.float32)
    bias_buf[...] = jnp.sum(terms[0] + terms[1], axis=0, keepdims=True)
    copies.append(pltpu.make_async_copy(bias_buf, bias_ref, sems.at[2]))
    copies[-1].start()
    for copy in copies:
        copy.wait()


def rounds_of(z_n):
    rounds = [1]
    while 2 * rounds[-1] < z_n // 2:
        rounds.append(2 * rounds[-1])
    return rounds


def pieces(dims):
    zh_n, tm_n = dims
    z_n, p_n = zh_n * Z_LO, tm_n // Z_LO
    chunk = ROWS // p_n
    piece = 16 * max(1, chunk // 16 // z_n)
    return chunk, piece, chunk // piece


def on_device(dims, inputs, clip_lengths, weight, bias, cotangent):
    zh_n, tm_n = dims
    z_n, p_n = zh_n * Z_LO, tm_n // Z_LO
    chunk, piece, owners = pieces(dims)
    block = inputs.shape
    dma = pltpu.SemaphoreType.DMA
    vmem, hbm = (pl.BlockSpec(memory_space=m) for m in (pltpu.VMEM, pltpu.HBM))
    operands = (clip_lengths, inputs, weight, bias.reshape(1, 128), cotangent)
    result, in_grad, full = pl.pallas_call(
        functools.partial(chip_kernel, dims),
        out_shape=(
            jax.ShapeDtypeStruct(block, jnp.bfloat16),
            jax.ShapeDtypeStruct(block, jnp.bfloat16),
            jax.ShapeDtypeStruct((2, ROWS, 128), jnp.bfloat16),
        ),
        in_specs=[hbm, hbm, hbm, hbm, hbm],
        out_specs=(vmem, vmem, vmem),
        scratch_shapes=[
            pltpu.SMEM(clip_lengths.shape, jnp.int32),
            pltpu.VMEM((1, 128), jnp.float32),
            pltpu.VMEM((4, 18, 32, 128), jnp.bfloat16),
            pltpu.VMEM((128, 512), jnp.float32),
            pltpu.VMEM((3, 3 * HALF, 1024), jnp.bfloat16),
            pltpu.VMEM((4, 18, 32, 128), jnp.bfloat16),
            pltpu.VMEM((3, 3, 3, 128, 128), jnp.bfloat16),
            pltpu.VMEM((2, 8, 32, 128), jnp.bfloat16),
            pltpu.VMEM((2, 256, 384), jnp.float32),
            pltpu.VMEM((ROWS, 128), jnp.bfloat16),
            pltpu.VMEM((p_n - 1, chunk, 128), jnp.bfloat16),
            pltpu.VMEM((chunk, 128), jnp.bfloat16),
            pltpu.VMEM((z_n - 1, piece, 128), jnp.bfloat16),
            pltpu.SemaphoreType.REGULAR((len(rounds_of(z_n)),)),
            dma((5,)), dma((6,)), dma((6,)), dma((4,)), dma((4,)),
            dma, dma, dma, dma, dma, dma((owners,)), dma, dma((p_n,)), dma, dma,
        ],
        compiler_params=pltpu.CompilerParams(
            collective_id=0, has_side_effects=True, vmem_limit_bytes=40 * 1024 * 1024
        ),
        name="chip_kernel",
    )(*(pltpu.with_memory_space_constraint(a, pltpu.HBM) for a in operands))
    result, in_grad, kern_grad, bias_grad = pl.pallas_call(
        functools.partial(finish_kernel, p_n),
        out_shape=(
            jax.ShapeDtypeStruct(block, jnp.bfloat16),
            jax.ShapeDtypeStruct(block, jnp.bfloat16),
            jax.ShapeDtypeStruct((3, 3, 3, 128, 128), jnp.float32),
            jax.ShapeDtypeStruct((1, 128), jnp.float32),
        ),
        in_specs=[vmem, vmem, vmem],
        out_specs=(hbm, hbm, hbm, hbm),
        scratch_shapes=[
            pltpu.VMEM((3, 3, 3, 128, 128), jnp.float32),
            pltpu.VMEM((1, 128), jnp.float32),
            dma((12,)),
        ],
        compiler_params=pltpu.CompilerParams(vmem_limit_bytes=32 * 1024 * 1024),
        name="finish_kernel",
    )(result, in_grad, full)
    return result, in_grad, kern_grad, bias_grad.reshape(128)


def solution(mesh):
    dims = (mesh.shape["dp"], mesh.shape["tm"])
    return jax.shard_map(
        functools.partial(on_device, dims),
        mesh=mesh,
        in_specs=(
            P("dp", "tm", "space", None, None),
            P("dp", None),
            P(),
            P(),
            P("dp", "tm", "space", None, None),
        ),
        out_specs=(
            P("dp", "tm", "space", None, None),
            P("dp", "tm", "space", None, None),
            P(),
            P(),
        ),
        check_vma=False,
    )
```

```python
import functools

import jax
import jax.numpy as jnp
from jax import lax
from jax.experimental import pallas as pl
from jax.experimental.pallas import tpu as pltpu
from jax.sharding import PartitionSpec as P

MESH = pl.DeviceIdType.MESH
Z_LO = 4
PLANE_Y = 4
HALF = 64
ROWS = 28 * HALF
TILES = 9 * HALF // 16


def tile_row(p_n, k, tile):
    chunk, per = ROWS // p_n, TILES // p_n
    if k < 3 and tile < per * p_n:
        return tile // per * chunk + (k * per + tile % per) * 16
    extra = k * (TILES - per * p_n) + (tile - per * p_n if k < 3 else tile)
    return extra % p_n * chunk + (3 * per + extra // p_n) * 16


def scalar_mask(ends, frame, lag):
    def clip(t):
        return sum((t >= end).astype(jnp.int32) for end in ends)

    earlier = frame - lag
    same = (clip(earlier) == clip(frame)) & (earlier >= 0)
    return same.astype(jnp.float32)


def scaled(values, mask):
    return values * jnp.full(values.shape, mask, jnp.float32).astype(values.dtype)


def column_sum(parts, back):
    count = parts.shape[0]
    col = lax.broadcasted_iota(jnp.int32, (count, 128), 0) % 32
    first, mid, last = parts[:, :128], parts[:, 128:256], parts[:, 256:]
    down, up = (last, first) if back else (first, last)
    down = jnp.where(col == 0, 0.0, pltpu.roll(down, 1, 0))
    up = jnp.where(col == 31, 0.0, pltpu.roll(up, count - 1, 0))
    return mid + down + up


def chip_kernel(
    dims, lens_hbm, x_hbm, w_hbm, bias_hbm, cot_hbm,
    out_ref, ig_ref, full,
    lens, bias, xs, xt, lt, dzs, wv, cotv, yacc, part, rsbuf, zs, zbuf,
    known, plane_known, pair_ready, loc, xsend, xrecv, dsend, drecv, rs_send, rs_recv, z_send, z_recv,
    zg_send, zg_recv, pg_send, pg_recv, cg_send, cg_recv,
):
    zh_n, tm_n = dims
    z_n, p_n = zh_n * Z_LO, tm_n // Z_LO
    chunk = ROWS // p_n
    rounds = rounds_of(z_n)

    dp, tm, core = lax.axis_index("dp"), lax.axis_index("tm"), lax.axis_index("space")
    other = 1 - core
    p, zl = tm // Z_LO, tm % Z_LO
    z = dp * Z_LO + zl
    after, before = (tm + 1) % tm_n, (tm + tm_n - 1) % tm_n

    def plane_dev(q):
        return (dp, q * Z_LO + zl, core)

    def z_dev(w):
        return (w // Z_LO, p * Z_LO + w % Z_LO, core)

    x_n = p_n // PLANE_Y
    xq = [(p // PLANE_Y + dx) % x_n * PLANE_Y for dx in range(x_n)]
    yq = [(p % PLANE_Y + dy) % PLANE_Y for dy in range(PLANE_Y)]
    far_first = sorted(
        ((dx, dy) for dx in range(x_n) for dy in range(PLANE_Y) if dx + dy),
        key=lambda d: -min(d[0], x_n - d[0]) - min(d[1], PLANE_Y - d[1]),
    )
    next_to = [xq[dx] + yq[0] for dx in (1, x_n - 1) if x_n > 1] + [xq[0] + yq[dy] for dy in (1, PLANE_Y - 1)]
    two_off = [xq[dx] + yq[0] for dx in range(2, x_n, x_n)] + [xq[0] + yq[dy] for dy in range(2, PLANE_Y, PLANE_Y)]

    barrier = pltpu.get_barrier_semaphore()

    def greet(device):
        pl.semaphore_signal(barrier, inc=1, device_id=device, device_id_type=MESH)

    def remote(src, dst, send, recv, device):
        return pltpu.make_async_remote_copy(
            src_ref=src, dst_ref=dst, send_sem=send, recv_sem=recv, device_id=device, device_id_type=MESH
        )

    own = pl.ds(1 + 8 * core, 8)
    edge_row = 7 * other
    edge = pl.ds(1 + 8 * core + edge_row, 1)
    inner = pl.ds(1 + 9 * core, 7)
    two, later = pl.ds(0, 2), pl.ds(2, 2)

    greet((dp, tm, other))
    for there, near in ((tm > 0, before), (tm < tm_n - 1, after)):
        @pl.when(there)
        def _():
            greet((dp, near, core))
            greet((dp, near, other))

    for q in next_to:
        greet(plane_dev(q))
    greet(z_dev((z + 1) % z_n))
    greet(z_dev((z + z_n - 1) % z_n))

    get_x = pltpu.make_async_copy(x_hbm.at[0], xs.at[later, own], loc.at[0])
    get_w = pltpu.make_async_copy(w_hbm, wv, loc.at[1])
    get_cot = pltpu.make_async_copy(cot_hbm.at[0], cotv, loc.at[2])
    get_lens = pltpu.make_async_copy(lens_hbm, lens, loc.at[3])
    get_bias = pltpu.make_async_copy(bias_hbm, bias, loc.at[4])
    for copy in (get_x, get_w, get_lens, get_cot, get_bias):
        copy.start()
    for f in range(4):
        for r in (0, 17):
            xs[f, r] = jnp.zeros((32, 128), jnp.bfloat16)
            dzs[f, r] = jnp.zeros((32, 128), jnp.bfloat16)

    @pl.when(tm == 0)
    def _():
        xs[two, pl.ds(1, 16)] = jnp.zeros((2, 16, 32, 128), jnp.bfloat16)

    @pl.when(tm == tm_n - 1)
    def _():
        dzs[later, pl.ds(1, 16)] = jnp.zeros((2, 16, 32, 128), jnp.bfloat16)

    get_lens.wait()
    ends = [lens[0, 0]]
    for j in range(1, lens.shape[1]):
        ends.append(ends[-1] + lens[0, j])
    base = 2 * tm
    m0 = [scalar_mask(ends, base + t, 2) for t in range(4)]
    m1 = [scalar_mask(ends, base + t, 1) for t in range(3)]

    get_x.wait()
    sides = (tm + tm_n - 1) // tm_n + (2 * (tm_n - 1) - tm) // tm_n
    pl.semaphore_wait(barrier, 1 + len(next_to) + 2 + 2 * sides)

    def tell_plane(r):
        for q in (next_to, two_off)[r]:
            pl.semaphore_signal(plane_known.at[r], inc=1, device_id=plane_dev(q), device_id_type=MESH)

    def hear_plane(r):
        if (next_to, two_off)[r]:
            pl.semaphore_wait(plane_known.at[r], len((next_to, two_off)[r]))

    def tell(r):
        for w in (z + rounds[r], z + z_n - rounds[r]):
            pl.semaphore_signal(known.at[r], inc=1, device_id=z_dev(w % z_n), device_id_type=MESH)

    def hear(r):
        pl.semaphore_wait(known.at[r], 2)

    tell_plane(0)
    tell(0)

    x_next = [
        remote(xs.at[2 + f, own], xs.at[f, own], xsend.at[1 + 4 * f], xrecv.at[1 + 4 * f], (dp, after, core))
        for f in range(2)
    ]
    x_edge = remote(
        xs.at[later, edge], xs.at[two, edge], xsend.at[2], xrecv.at[2], (dp, after, other)
    )
    x_pair = remote(xs.at[later, own], xs.at[later, own], xsend.at[0], xrecv.at[0], (dp, tm, other))
    x_fwd = [
        remote(xs.at[f, inner], xs.at[f, inner], xsend.at[3 + f], xrecv.at[3 + f], (dp, tm, other))
        for f in range(2)
    ]

    @pl.when(tm < tm_n - 1)
    def _():
        x_edge.start()
        x_next[1].start()
        x_next[0].start()

    x_pair.start()

    def x_rows(f):
        return jnp.concatenate(
            [xs[f, pl.ds(8 * core + a, 8)].reshape(256, 128) for a in range(3)], axis=1
        )

    def w_fwd(k):
        return jnp.concatenate(
            [jnp.concatenate([wv[k, a, b] for b in range(3)], axis=1) for a in range(3)], axis=0
        )

    def mm(lhs, rhs):
        return jnp.dot(lhs, rhs, preferred_element_type=jnp.float32)

    def turned(f):
        xt[...] = xs[f, pl.ds(1, 16)].reshape(512, 128).astype(jnp.float32).T
        mid = xt[pl.ds(pl.multiple_of(HALF * core, HALF), HALF), :]
        col = lax.broadcasted_iota(jnp.int32, (HALF, 512), 1) % 32
        left = jnp.where(col == 0, 0.0, pltpu.roll(mid, 1, 1))
        right = jnp.where(col == 31, 0.0, pltpu.roll(mid, 511, 1))
        block = jnp.concatenate([left, mid, right], axis=0)
        for t in range(2):
            k = f - t
            if k < 0 or k > 2:
                continue
            kept = block if k == 2 else block * (m1[t] if k == 1 else m0[t])
            lt[k, :, pl.ds(512 * t, 512)] = kept.astype(jnp.bfloat16)

    get_w.wait()
    x_pair.wait_recv()
    yacc[0] = mm(x_rows(2), w_fwd(2))
    yacc[1] = mm(
        jnp.concatenate([x_rows(3), scaled(x_rows(2), m1[1])], axis=1),
        jnp.concatenate([w_fwd(2), w_fwd(1)], axis=0),
    )
    turned(2)
    turned(3)
    get_cot.wait()
    get_bias.wait()

    def halo_frame(f):
        @pl.when(tm > 0)
        def _():
            x_next[f].wait_recv()
            x_fwd[f].start()

    def finish_frame(f):
        zed = column_sum(yacc[f], False) + bias[...]
        sig = jax.nn.sigmoid(zed)
        out_ref[0, f] = (zed * sig).astype(jnp.bfloat16).reshape(8, 32, 128)
        cot = cotv[f].reshape(256, 128).astype(jnp.float32)
        dz = (cot * sig * (1.0 + zed * (1.0 - sig))).astype(jnp.bfloat16)
        dzs[f, own] = dz.reshape(8, 32, 128)
        d_pair[f].start()
        return jnp.sum(dz.astype(jnp.float32).reshape(16, 16, 128), axis=0)

    d_pair = [
        remote(dzs.at[f, own], dzs.at[f, own], dsend.at[3 * f], drecv.at[3 * f], (dp, tm, other))
        for f in range(2)
    ]

    hear_plane(0)
    tell_plane(1)
    pl.when(tm > 0)(x_edge.wait_recv)
    halo_frame(1)
    yacc[0] += mm(scaled(x_rows(1), m1[0]), w_fwd(1))
    yacc[1] += mm(scaled(x_rows(1), m0[1]), w_fwd(0))
    bias_part = finish_frame(1)
    halo_frame(0)
    yacc[0] += mm(scaled(x_rows(0), m0[0]), w_fwd(0))
    bias_part += finish_frame(0)

    d_next = remote(dzs.at[two, own], dzs.at[later, own], dsend.at[1], drecv.at[1], (dp, before, core))
    d_edge = remote(dzs.at[two, edge], dzs.at[later, edge], dsend.at[2], drecv.at[2], (dp, before, other))

    early, middle = dp < zh_n // 2, dp == zh_n // 2
    near = zl > 0

    def d_start():
        d_next.start()
        d_edge.start()

    pl.when(near | (early & (tm > 0)))(d_start)

    part[pl.ds(tile_row(p_n, 3, 0), 16), :] = bias_part.astype(jnp.bfloat16)
    for spare in range(1, ROWS // 16 - 3 * TILES):
        part[pl.ds(tile_row(p_n, 3, spare), 16), :] = jnp.zeros((16, 128), jnp.bfloat16)
    for f in (1, 0):
        pl.when(tm > 0)(x_fwd[f].wait_recv)
        turned(f)
    d_pair[1].wait_recv()
    d_pair[0].wait_recv()

    right_side = jnp.concatenate(
        [
            jnp.concatenate([dzs[t, pl.ds(2 - a, 16)].reshape(512, 128) for a in range(3)], axis=1)
            for t in range(2)
        ],
        axis=0,
    )

    def chunk_rows(q):
        return pl.ds(pl.multiple_of(q * chunk, 16), chunk)

    per = TILES // p_n * 16
    for k in range(3):
        grad = mm(lt[k], right_side)
        for a in range(3):
            for b in range(3):
                for j in range(HALF // 16):
                    block = grad[b * HALF + j * 16 : b * HALF + j * 16 + 16, a * 128 : (a + 1) * 128]
                    row = tile_row(p_n, k, (a * 3 + b) * (HALF // 16) + j)
                    part[pl.ds(row, 16), :] = block.astype(jnp.bfloat16)
        count = per if k < 2 else chunk - 2 * per
        if k == 0:
            hear_plane(1)

        for dx, dy in far_first:
            q = xq[dx] + yq[dy]
            remote(
                part.at[pl.ds(pl.multiple_of(q * chunk + k * per, 16), count)],
                rsbuf.at[dx * PLANE_Y + dy - 1, pl.ds(k * per, count)], rs_send, rs_recv, plane_dev(q),
            ).start()

    hear(0)
    if len(rounds) > 1:
        tell(1)

    def d_rows(f):
        return jnp.concatenate(
            [dzs[f, pl.ds(8 * core + 2 - a, 8)].reshape(256, 128) for a in range(3)], axis=1
        )

    def w_back(k):
        return jnp.concatenate([wv[k, a].reshape(384, 128) for a in range(3)], axis=1)

    def mm_t(lhs, rhs):
        return lax.dot_general(lhs, rhs, (((1,), (1,)), ((), ())), preferred_element_type=jnp.float32)

    yacc[0] = mm_t(
        jnp.concatenate([d_rows(0), scaled(d_rows(1), m1[1])], axis=1),
        jnp.concatenate([w_back(2), w_back(1)], axis=1),
    )
    yacc[1] = mm_t(d_rows(1), w_back(2))

    for r in range(1, len(rounds) - 1):
        hear(r)
        tell(r + 1)

    remote(rsbuf, rsbuf, rs_send, rs_recv, plane_dev(p)).wait_recv()
    total = part[chunk_rows(p), :].astype(jnp.float32)
    for q in range(p_n - 1):
        total += rsbuf[q].astype(jnp.float32)
    zs[...] = total.astype(jnp.bfloat16)

    if len(rounds) > 1:
        hear(len(rounds) - 1)

    to_first = remote(zs, zbuf.at[(z + z_n - 1) % z_n], z_send, z_recv, z_dev(z * 0))
    pl.when(z > 0)(to_first.start)
    pl.when(jnp.logical_not(near) & middle & (tm > 0))(d_start)

    def rest_of_in_grad():
        @pl.when(tm < tm_n - 1)
        def _():
            d_next.wait_recv()
            d_edge.wait_recv()

        yacc[0] += mm_t(scaled(d_rows(2), m0[2]), w_back(0))
        yacc[1] += mm_t(
            jnp.concatenate([scaled(d_rows(2), m1[2]), scaled(d_rows(3), m0[3])], axis=1),
            jnp.concatenate([w_back(1), w_back(0)], axis=1),
        )
        for f in range(2):
            ig_ref[0, f] = column_sum(yacc[f], True).astype(jnp.bfloat16).reshape(8, 32, 128)

    pl.when(early | middle)(rest_of_in_grad)

    half = z_n // 2
    mine = full.at[core, chunk_rows(p)]

    def z_share(w):
        remote(mine, mine, zg_send, zg_recv, z_dev(w)).start()

    @pl.when(z == 0)
    def _():
        remote(zbuf, zbuf, z_send, z_recv, z_dev(z)).wait_recv()
        acc = zs[...].astype(jnp.float32)
        for w in range(z_n - 1):
            acc += zbuf[w].astype(jnp.float32)
        full[core, chunk_rows(p), :] = acc.astype(jnp.bfloat16)
        for w in range(1, min(4, half)):
            z_share(w)
        pl.semaphore_signal(pair_ready, inc=1, device_id=(dp, tm, other), device_id_type=MESH)

    pl.when(z > 0)(lambda: remote(mine, mine, zg_send, zg_recv, z_dev(z)).wait_recv())

    @pl.when(z == z_n - 1)
    def _():
        for w in range(half, z_n - 1):
            z_share(w)

    for dx, dy in far_first:
        remote(mine, mine, pg_send, pg_recv.at[p], plane_dev(xq[dx] + yq[dy])).start()

    @pl.when(z == 0)
    def _():
        pl.semaphore_wait(pair_ready, 1)
        for w in (*range(4, half), z_n - 1):
            z_share(w)

    pl.when(jnp.logical_not(near | early | middle) & (tm > 0))(d_start)

    def cg_copy(rows):
        return remote(full.at[core, rows], full.at[core, rows], cg_send, cg_recv, (dp, tm, other))

    cg_copy(chunk_rows(p)).start()

    @pl.loop(1, p_n)
    def _(i):
        q = (p + i) % p_n
        rows = chunk_rows(q)
        remote(full.at[core, rows], full.at[core, rows], pg_send, pg_recv.at[q], plane_dev(q)).wait_recv()
        cg_copy(rows).start()

    pl.when(jnp.logical_not(early | middle))(rest_of_in_grad)

    @pl.when(tm < tm_n - 1)
    def _():
        x_next[0].wait_send()
        x_next[1].wait_send()
        x_edge.wait_send()

    x_pair.wait_send()
    d_pair[0].wait_send()
    d_pair[1].wait_send()

    @pl.when(tm > 0)
    def _():
        x_fwd[0].wait_send()
        x_fwd[1].wait_send()
        d_next.wait_send()
        d_edge.wait_send()

    rest = pl.ds(0, (p_n - 1) * chunk)
    remote(part.at[rest], part.at[rest], rs_send, rs_recv, plane_dev(p)).wait_send()

    pl.when(z > 0)(to_first.wait_send)
    for w, count in ((0, half), (z_n - 1, half - 1)):
        if count:
            sent = zbuf.at[pl.ds(0, count)]
            pl.when(z == w)(remote(sent, sent, zg_send, z_recv, z_dev(z)).wait_send)

    remote(full.at[core, rest], full.at[core, rest], pg_send, pg_recv.at[p], plane_dev(p)).wait_send()
    everything = remote(full.at[core], full.at[other], cg_send, cg_recv, (dp, tm, other))
    everything.wait_send()
    everything.wait_recv()


def finish_kernel(p_n, out_in, ig_in, full, out_ref, ig_ref, grad_ref, bias_ref, buf, bias_buf, sems):
    copies = [
        pltpu.make_async_copy(out_in, out_ref, sems.at[0]),
        pltpu.make_async_copy(ig_in, ig_ref, sems.at[1]),
    ]
    for k in range(3):
        for a in range(3):
            for b in range(3):
                for side in range(2):
                    for j in range(HALF // 16):
                        row = tile_row(p_n, k, (a * 3 + b) * (HALF // 16) + j)
                        buf[k, a, b, pl.ds(side * HALF + j * 16, 16), :] = full[
                            side, pl.ds(row, 16), :
                        ].astype(jnp.float32)
            copies.append(pltpu.make_async_copy(buf.at[k, a], grad_ref.at[k, a], sems.at[3 + 3 * k + a]))
            copies[-1].start()
    copies[0].start()
    copies[1].start()
    terms = full[:, pl.ds(tile_row(p_n, 3, 0), 16), :].astype(jnp.float32)
    bias_buf[...] = jnp.sum(terms[0] + terms[1], axis=0, keepdims=True)
    copies.append(pltpu.make_async_copy(bias_buf, bias_ref, sems.at[2]))
    copies[-1].start()
    for copy in copies:
        copy.wait()


def rounds_of(z_n):
    rounds = [1]
    while 2 * rounds[-1] < z_n // 2:
        rounds.append(2 * rounds[-1])
    return rounds


def on_device(dims, inputs, clip_lengths, weight, bias, cotangent):
    zh_n, tm_n = dims
    z_n, p_n = zh_n * Z_LO, tm_n // Z_LO
    chunk = ROWS // p_n
    block = inputs.shape
    dma = pltpu.SemaphoreType.DMA
    vmem, hbm = (pl.BlockSpec(memory_space=m) for m in (pltpu.VMEM, pltpu.HBM))
    operands = (clip_lengths, inputs, weight, bias.reshape(1, 128), cotangent)
    result, in_grad, full = pl.pallas_call(
        functools.partial(chip_kernel, dims),
        out_shape=(
            jax.ShapeDtypeStruct(block, jnp.bfloat16),
            jax.ShapeDtypeStruct(block, jnp.bfloat16),
            jax.ShapeDtypeStruct((2, ROWS, 128), jnp.bfloat16),
        ),
        in_specs=[hbm, hbm, hbm, hbm, hbm],
        out_specs=(vmem, vmem, vmem),
        scratch_shapes=[
            pltpu.SMEM(clip_lengths.shape, jnp.int32),
            pltpu.VMEM((1, 128), jnp.float32),
            pltpu.VMEM((4, 18, 32, 128), jnp.bfloat16),
            pltpu.VMEM((128, 512), jnp.float32),
            pltpu.VMEM((3, 3 * HALF, 1024), jnp.bfloat16),
            pltpu.VMEM((4, 18, 32, 128), jnp.bfloat16),
            pltpu.VMEM((3, 3, 3, 128, 128), jnp.bfloat16),
            pltpu.VMEM((2, 8, 32, 128), jnp.bfloat16),
            pltpu.VMEM((2, 256, 384), jnp.float32),
            pltpu.VMEM((ROWS, 128), jnp.bfloat16),
            pltpu.VMEM((p_n - 1, chunk, 128), jnp.bfloat16),
            pltpu.VMEM((chunk, 128), jnp.bfloat16),
            pltpu.VMEM((z_n - 1, chunk, 128), jnp.bfloat16),
            pltpu.SemaphoreType.REGULAR((len(rounds_of(z_n)),)),
            pltpu.SemaphoreType.REGULAR((2,)),
            pltpu.SemaphoreType.REGULAR,
            dma((5,)), dma((6,)), dma((6,)), dma((4,)), dma((4,)),
            dma, dma, dma, dma, dma, dma, dma, dma((p_n,)), dma, dma,
        ],
        compiler_params=pltpu.CompilerParams(
            collective_id=0, has_side_effects=True, vmem_limit_bytes=40 * 1024 * 1024
        ),
        name="chip_kernel",
    )(*(pltpu.with_memory_space_constraint(a, pltpu.HBM) for a in operands))
    result, in_grad, kern_grad, bias_grad = pl.pallas_call(
        functools.partial(finish_kernel, p_n),
        out_shape=(
            jax.ShapeDtypeStruct(block, jnp.bfloat16),
            jax.ShapeDtypeStruct(block, jnp.bfloat16),
            jax.ShapeDtypeStruct((3, 3, 3, 128, 128), jnp.float32),
            jax.ShapeDtypeStruct((1, 128), jnp.float32),
        ),
        in_specs=[vmem, vmem, vmem],
        out_specs=(hbm, hbm, hbm, hbm),
        scratch_shapes=[
            pltpu.VMEM((3, 3, 3, 128, 128), jnp.float32),
            pltpu.VMEM((1, 128), jnp.float32),
            dma((12,)),
        ],
        compiler_params=pltpu.CompilerParams(vmem_limit_bytes=32 * 1024 * 1024),
        name="finish_kernel",
    )(result, in_grad, full)
    return result, in_grad, kern_grad, bias_grad.reshape(128)


def solution(mesh):
    dims = (mesh.shape["dp"], mesh.shape["tm"])
    return jax.shard_map(
        functools.partial(on_device, dims),
        mesh=mesh,
        in_specs=(
            P("dp", "tm", "space", None, None),
            P("dp", None),
            P(),
            P(),
            P("dp", "tm", "space", None, None),
        ),
        out_specs=(
            P("dp", "tm", "space", None, None),
            P("dp", "tm", "space", None, None),
            P(),
            P(),
        ),
        check_vma=False,
    )
```

```python
import functools

import jax
import jax.numpy as jnp
from jax import lax
from jax.experimental import pallas as pl
from jax.experimental.pallas import tpu as pltpu
from jax.sharding import PartitionSpec as P

MESH = pl.DeviceIdType.MESH
Z_LO = 4
PLANE_Y = 4
HALF = 64
ROWS = 28 * HALF
TILES = 9 * HALF // 16


def tile_row(p_n, k, tile):
    chunk, per = ROWS // p_n, TILES // p_n
    if k < 3 and tile < per * p_n:
        return tile // per * chunk + (k * per + tile % per) * 16
    extra = k * (TILES - per * p_n) + (tile - per * p_n if k < 3 else tile)
    return extra % p_n * chunk + (3 * per + extra // p_n) * 16


def scalar_mask(ends, frame, lag):
    def clip(t):
        return sum((t >= end).astype(jnp.int32) for end in ends)

    earlier = frame - lag
    same = (clip(earlier) == clip(frame)) & (earlier >= 0)
    return same.astype(jnp.float32)


def scaled(values, mask):
    return values * jnp.full(values.shape, mask, jnp.float32).astype(values.dtype)


def column_sum(parts, back):
    count = parts.shape[0]
    col = lax.broadcasted_iota(jnp.int32, (count, 128), 0) % 32
    first, mid, last = parts[:, :128], parts[:, 128:256], parts[:, 256:]
    down, up = (last, first) if back else (first, last)
    down = jnp.where(col == 0, 0.0, pltpu.roll(down, 1, 0))
    up = jnp.where(col == 31, 0.0, pltpu.roll(up, count - 1, 0))
    return mid + down + up


def chip_kernel(
    dims, lens_hbm, x_hbm, w_hbm, bias_hbm, cot_hbm,
    out_ref, ig_ref, full,
    lens, bias, xs, xt, lt, dzs, wv, cotv, yacc, part, rsbuf, zs, zbuf,
    known, plane_known, loc, xsend, xrecv, dsend, drecv, rs_send, rs_recv, z_send, z_recv,
    zg_send, zg_recv, pg_send, pg_recv, cg_send, cg_recv,
):
    zh_n, tm_n = dims
    z_n, p_n = zh_n * Z_LO, tm_n // Z_LO
    chunk = ROWS // p_n
    rounds = rounds_of(z_n)

    dp, tm, core = lax.axis_index("dp"), lax.axis_index("tm"), lax.axis_index("space")
    other = 1 - core
    p, zl = tm // Z_LO, tm % Z_LO
    z = dp * Z_LO + zl
    after, before = (tm + 1) % tm_n, (tm + tm_n - 1) % tm_n

    def plane_dev(q):
        return (dp, q * Z_LO + zl, core)

    def z_dev(w):
        return (w // Z_LO, p * Z_LO + w % Z_LO, core)

    x_n = p_n // PLANE_Y
    xq = [(p // PLANE_Y + dx) % x_n * PLANE_Y for dx in range(x_n)]
    yq = [(p % PLANE_Y + dy) % PLANE_Y for dy in range(PLANE_Y)]
    far_first = sorted(
        ((dx, dy) for dx in range(x_n) for dy in range(PLANE_Y) if dx + dy),
        key=lambda d: -min(d[0], x_n - d[0]) - min(d[1], PLANE_Y - d[1]),
    )
    next_to = [xq[dx] + yq[0] for dx in (1, x_n - 1) if x_n > 1] + [xq[0] + yq[dy] for dy in (1, PLANE_Y - 1)]
    two_off = [xq[dx] + yq[0] for dx in range(2, x_n, x_n)] + [xq[0] + yq[dy] for dy in range(2, PLANE_Y, PLANE_Y)]

    barrier = pltpu.get_barrier_semaphore()

    def greet(device):
        pl.semaphore_signal(barrier, inc=1, device_id=device, device_id_type=MESH)

    def remote(src, dst, send, recv, device):
        return pltpu.make_async_remote_copy(
            src_ref=src, dst_ref=dst, send_sem=send, recv_sem=recv, device_id=device, device_id_type=MESH
        )

    own = pl.ds(1 + 8 * core, 8)
    edge_row = 7 * other
    edge = pl.ds(1 + 8 * core + edge_row, 1)
    inner = pl.ds(1 + 9 * core, 7)
    two, later = pl.ds(0, 2), pl.ds(2, 2)

    greet((dp, tm, other))
    for there, near in ((tm > 0, before), (tm < tm_n - 1, after)):
        @pl.when(there)
        def _():
            greet((dp, near, core))
            greet((dp, near, other))

    for q in next_to:
        greet(plane_dev(q))
    greet(z_dev((z + 1) % z_n))
    greet(z_dev((z + z_n - 1) % z_n))

    get_x = pltpu.make_async_copy(x_hbm.at[0], xs.at[later, own], loc.at[0])
    get_w = pltpu.make_async_copy(w_hbm, wv, loc.at[1])
    get_cot = pltpu.make_async_copy(cot_hbm.at[0], cotv, loc.at[2])
    get_lens = pltpu.make_async_copy(lens_hbm, lens, loc.at[3])
    get_bias = pltpu.make_async_copy(bias_hbm, bias, loc.at[4])
    for copy in (get_x, get_w, get_lens, get_cot, get_bias):
        copy.start()
    for f in range(4):
        for r in (0, 17):
            xs[f, r] = jnp.zeros((32, 128), jnp.bfloat16)
            dzs[f, r] = jnp.zeros((32, 128), jnp.bfloat16)

    @pl.when(tm == 0)
    def _():
        xs[two, pl.ds(1, 16)] = jnp.zeros((2, 16, 32, 128), jnp.bfloat16)

    @pl.when(tm == tm_n - 1)
    def _():
        dzs[later, pl.ds(1, 16)] = jnp.zeros((2, 16, 32, 128), jnp.bfloat16)

    get_lens.wait()
    ends = [lens[0, 0]]
    for j in range(1, lens.shape[1]):
        ends.append(ends[-1] + lens[0, j])
    base = 2 * tm
    m0 = [scalar_mask(ends, base + t, 2) for t in range(4)]
    m1 = [scalar_mask(ends, base + t, 1) for t in range(3)]

    get_x.wait()
    sides = (tm + tm_n - 1) // tm_n + (2 * (tm_n - 1) - tm) // tm_n
    pl.semaphore_wait(barrier, 1 + len(next_to) + 2 + 2 * sides)

    def tell_plane(r):
        for q in (next_to, two_off)[r]:
            pl.semaphore_signal(plane_known.at[r], inc=1, device_id=plane_dev(q), device_id_type=MESH)

    def hear_plane(r):
        if (next_to, two_off)[r]:
            pl.semaphore_wait(plane_known.at[r], len((next_to, two_off)[r]))

    def tell(r):
        for w in (z + rounds[r], z + z_n - rounds[r]):
            pl.semaphore_signal(known.at[r], inc=1, device_id=z_dev(w % z_n), device_id_type=MESH)

    def hear(r):
        pl.semaphore_wait(known.at[r], 2)

    tell_plane(0)
    tell(0)

    x_next = [
        remote(xs.at[2 + f, own], xs.at[f, own], xsend.at[1 + 4 * f], xrecv.at[1 + 4 * f], (dp, after, core))
        for f in range(2)
    ]
    x_edge = remote(
        xs.at[later, edge], xs.at[two, edge], xsend.at[2], xrecv.at[2], (dp, after, other)
    )
    x_pair = remote(xs.at[later, own], xs.at[later, own], xsend.at[0], xrecv.at[0], (dp, tm, other))
    x_fwd = [
        remote(xs.at[f, inner], xs.at[f, inner], xsend.at[3 + f], xrecv.at[3 + f], (dp, tm, other))
        for f in range(2)
    ]

    @pl.when(tm < tm_n - 1)
    def _():
        x_edge.start()
        x_next[1].start()
        x_next[0].start()

    x_pair.start()

    def x_rows(f):
        return jnp.concatenate(
            [xs[f, pl.ds(8 * core + a, 8)].reshape(256, 128) for a in range(3)], axis=1
        )

    def w_fwd(k):
        return jnp.concatenate(
            [jnp.concatenate([wv[k, a, b] for b in range(3)], axis=1) for a in range(3)], axis=0
        )

    def mm(lhs, rhs):
        return jnp.dot(lhs, rhs, preferred_element_type=jnp.float32)

    def turned(f):
        xt[...] = xs[f, pl.ds(1, 16)].reshape(512, 128).astype(jnp.float32).T
        mid = xt[pl.ds(pl.multiple_of(HALF * core, HALF), HALF), :]
        col = lax.broadcasted_iota(jnp.int32, (HALF, 512), 1) % 32
        left = jnp.where(col == 0, 0.0, pltpu.roll(mid, 1, 1))
        right = jnp.where(col == 31, 0.0, pltpu.roll(mid, 511, 1))
        block = jnp.concatenate([left, mid, right], axis=0)
        for t in range(2):
            k = f - t
            if k < 0 or k > 2:
                continue
            kept = block if k == 2 else block * (m1[t] if k == 1 else m0[t])
            lt[k, :, pl.ds(512 * t, 512)] = kept.astype(jnp.bfloat16)

    get_w.wait()
    x_pair.wait_recv()
    yacc[0] = mm(x_rows(2), w_fwd(2))
    yacc[1] = mm(
        jnp.concatenate([x_rows(3), scaled(x_rows(2), m1[1])], axis=1),
        jnp.concatenate([w_fwd(2), w_fwd(1)], axis=0),
    )
    turned(2)
    turned(3)
    get_cot.wait()
    get_bias.wait()

    def halo_frame(f):
        @pl.when(tm > 0)
        def _():
            x_next[f].wait_recv()
            x_fwd[f].start()

    def finish_frame(f):
        zed = column_sum(yacc[f], False) + bias[...]
        sig = jax.nn.sigmoid(zed)
        out_ref[0, f] = (zed * sig).astype(jnp.bfloat16).reshape(8, 32, 128)
        cot = cotv[f].reshape(256, 128).astype(jnp.float32)
        dz = (cot * sig * (1.0 + zed * (1.0 - sig))).astype(jnp.bfloat16)
        dzs[f, own] = dz.reshape(8, 32, 128)
        d_pair[f].start()
        return jnp.sum(dz.astype(jnp.float32).reshape(16, 16, 128), axis=0)

    d_pair = [
        remote(dzs.at[f, own], dzs.at[f, own], dsend.at[3 * f], drecv.at[3 * f], (dp, tm, other))
        for f in range(2)
    ]

    hear_plane(0)
    tell_plane(1)
    pl.when(tm > 0)(x_edge.wait_recv)
    halo_frame(1)
    yacc[0] += mm(scaled(x_rows(1), m1[0]), w_fwd(1))
    yacc[1] += mm(scaled(x_rows(1), m0[1]), w_fwd(0))
    bias_part = finish_frame(1)
    halo_frame(0)
    yacc[0] += mm(scaled(x_rows(0), m0[0]), w_fwd(0))
    bias_part += finish_frame(0)

    d_next = remote(dzs.at[two, own], dzs.at[later, own], dsend.at[1], drecv.at[1], (dp, before, core))
    d_edge = remote(dzs.at[two, edge], dzs.at[later, edge], dsend.at[2], drecv.at[2], (dp, before, other))

    early, middle = dp < zh_n // 2, dp == zh_n // 2
    near = zl > 0

    def d_start():
        d_next.start()
        d_edge.start()

    pl.when(near | (early & (tm > 0)))(d_start)

    part[pl.ds(tile_row(p_n, 3, 0), 16), :] = bias_part.astype(jnp.bfloat16)
    for spare in range(1, ROWS // 16 - 3 * TILES):
        part[pl.ds(tile_row(p_n, 3, spare), 16), :] = jnp.zeros((16, 128), jnp.bfloat16)
    for f in (1, 0):
        pl.when(tm > 0)(x_fwd[f].wait_recv)
        turned(f)
    d_pair[1].wait_recv()
    d_pair[0].wait_recv()

    right_side = jnp.concatenate(
        [
            jnp.concatenate([dzs[t, pl.ds(2 - a, 16)].reshape(512, 128) for a in range(3)], axis=1)
            for t in range(2)
        ],
        axis=0,
    )

    def chunk_rows(q):
        return pl.ds(pl.multiple_of(q * chunk, 16), chunk)

    per = TILES // p_n * 16
    for k in range(3):
        grad = mm(lt[k], right_side)
        for a in range(3):
            for b in range(3):
                for j in range(HALF // 16):
                    block = grad[b * HALF + j * 16 : b * HALF + j * 16 + 16, a * 128 : (a + 1) * 128]
                    row = tile_row(p_n, k, (a * 3 + b) * (HALF // 16) + j)
                    part[pl.ds(row, 16), :] = block.astype(jnp.bfloat16)
        count = per if k < 2 else chunk - 2 * per
        if k == 0:
            hear_plane(1)

        for dx, dy in far_first:
            q = xq[dx] + yq[dy]
            remote(
                part.at[pl.ds(pl.multiple_of(q * chunk + k * per, 16), count)],
                rsbuf.at[dx * PLANE_Y + dy - 1, pl.ds(k * per, count)], rs_send, rs_recv, plane_dev(q),
            ).start()

    hear(0)
    if len(rounds) > 1:
        tell(1)

    def d_rows(f):
        return jnp.concatenate(
            [dzs[f, pl.ds(8 * core + 2 - a, 8)].reshape(256, 128) for a in range(3)], axis=1
        )

    def w_back(k):
        return jnp.concatenate([wv[k, a].reshape(384, 128) for a in range(3)], axis=1)

    def mm_t(lhs, rhs):
        return lax.dot_general(lhs, rhs, (((1,), (1,)), ((), ())), preferred_element_type=jnp.float32)

    yacc[0] = mm_t(
        jnp.concatenate([d_rows(0), scaled(d_rows(1), m1[1])], axis=1),
        jnp.concatenate([w_back(2), w_back(1)], axis=1),
    )
    yacc[1] = mm_t(d_rows(1), w_back(2))

    for r in range(1, len(rounds) - 1):
        hear(r)
        tell(r + 1)

    remote(rsbuf, rsbuf, rs_send, rs_recv, plane_dev(p)).wait_recv()
    total = part[chunk_rows(p), :].astype(jnp.float32)
    for q in range(p_n - 1):
        total += rsbuf[q].astype(jnp.float32)
    zs[...] = total.astype(jnp.bfloat16)

    if len(rounds) > 1:
        hear(len(rounds) - 1)

    to_first = remote(zs, zbuf.at[(z + z_n - 1) % z_n], z_send, z_recv, z_dev(z * 0))
    pl.when(z > 0)(to_first.start)
    pl.when(jnp.logical_not(near) & middle & (tm > 0))(d_start)

    def rest_of_in_grad():
        @pl.when(tm < tm_n - 1)
        def _():
            d_next.wait_recv()
            d_edge.wait_recv()

        yacc[0] += mm_t(scaled(d_rows(2), m0[2]), w_back(0))
        yacc[1] += mm_t(
            jnp.concatenate([scaled(d_rows(2), m1[2]), scaled(d_rows(3), m0[3])], axis=1),
            jnp.concatenate([w_back(1), w_back(0)], axis=1),
        )
        for f in range(2):
            ig_ref[0, f] = column_sum(yacc[f], True).astype(jnp.bfloat16).reshape(8, 32, 128)

    pl.when(early | middle)(rest_of_in_grad)

    half = z_n // 2
    mine = full.at[core, chunk_rows(p)]

    def z_share(w):
        remote(mine, mine, zg_send, zg_recv, z_dev(w)).start()

    @pl.when(z == 0)
    def _():
        remote(zbuf, zbuf, z_send, z_recv, z_dev(z)).wait_recv()
        acc = zs[...].astype(jnp.float32)
        for w in range(z_n - 1):
            acc += zbuf[w].astype(jnp.float32)
        full[core, chunk_rows(p), :] = acc.astype(jnp.bfloat16)
        for w in (*range(1, half), z_n - 1):
            z_share(w)

    pl.when(z > 0)(lambda: remote(mine, mine, zg_send, zg_recv, z_dev(z)).wait_recv())

    @pl.when(z == z_n - 1)
    def _():
        for w in range(half, z_n - 1):
            z_share(w)

    for dx, dy in far_first:
        remote(mine, mine, pg_send, pg_recv.at[p], plane_dev(xq[dx] + yq[dy])).start()


    pl.when(jnp.logical_not(near | early | middle) & (tm > 0))(d_start)

    def cg_copy(rows):
        return remote(full.at[core, rows], full.at[core, rows], cg_send, cg_recv, (dp, tm, other))

    cg_copy(chunk_rows(p)).start()

    @pl.loop(1, p_n)
    def _(i):
        q = (p + i) % p_n
        rows = chunk_rows(q)
        remote(full.at[core, rows], full.at[core, rows], pg_send, pg_recv.at[q], plane_dev(q)).wait_recv()
        cg_copy(rows).start()

    pl.when(jnp.logical_not(early | middle))(rest_of_in_grad)

    @pl.when(tm < tm_n - 1)
    def _():
        x_next[0].wait_send()
        x_next[1].wait_send()
        x_edge.wait_send()

    x_pair.wait_send()
    d_pair[0].wait_send()
    d_pair[1].wait_send()

    @pl.when(tm > 0)
    def _():
        x_fwd[0].wait_send()
        x_fwd[1].wait_send()
        d_next.wait_send()
        d_edge.wait_send()

    rest = pl.ds(0, (p_n - 1) * chunk)
    remote(part.at[rest], part.at[rest], rs_send, rs_recv, plane_dev(p)).wait_send()

    pl.when(z > 0)(to_first.wait_send)
    for w, count in ((0, half), (z_n - 1, half - 1)):
        if count:
            sent = zbuf.at[pl.ds(0, count)]
            pl.when(z == w)(remote(sent, sent, zg_send, z_recv, z_dev(z)).wait_send)

    remote(full.at[core, rest], full.at[core, rest], pg_send, pg_recv.at[p], plane_dev(p)).wait_send()
    everything = remote(full.at[core], full.at[other], cg_send, cg_recv, (dp, tm, other))
    everything.wait_send()
    everything.wait_recv()


def finish_kernel(p_n, out_in, ig_in, full, out_ref, ig_ref, grad_ref, bias_ref, buf, bias_buf, sems):
    copies = [
        pltpu.make_async_copy(out_in, out_ref, sems.at[0]),
        pltpu.make_async_copy(ig_in, ig_ref, sems.at[1]),
    ]
    for k in range(3):
        for a in range(3):
            for b in range(3):
                for side in range(2):
                    for j in range(HALF // 16):
                        row = tile_row(p_n, k, (a * 3 + b) * (HALF // 16) + j)
                        buf[k, a, b, pl.ds(side * HALF + j * 16, 16), :] = full[
                            side, pl.ds(row, 16), :
                        ].astype(jnp.float32)
            copies.append(pltpu.make_async_copy(buf.at[k, a], grad_ref.at[k, a], sems.at[3 + 3 * k + a]))
            copies[-1].start()
    copies[0].start()
    copies[1].start()
    terms = full[:, pl.ds(tile_row(p_n, 3, 0), 16), :].astype(jnp.float32)
    bias_buf[...] = jnp.sum(terms[0] + terms[1], axis=0, keepdims=True)
    copies.append(pltpu.make_async_copy(bias_buf, bias_ref, sems.at[2]))
    copies[-1].start()
    for copy in copies:
        copy.wait()


def rounds_of(z_n):
    rounds = [1]
    while 2 * rounds[-1] < z_n // 2:
        rounds.append(2 * rounds[-1])
    return rounds


def on_device(dims, inputs, clip_lengths, weight, bias, cotangent):
    zh_n, tm_n = dims
    z_n, p_n = zh_n * Z_LO, tm_n // Z_LO
    chunk = ROWS // p_n
    block = inputs.shape
    dma = pltpu.SemaphoreType.DMA
    vmem, hbm = (pl.BlockSpec(memory_space=m) for m in (pltpu.VMEM, pltpu.HBM))
    operands = (clip_lengths, inputs, weight, bias.reshape(1, 128), cotangent)
    result, in_grad, full = pl.pallas_call(
        functools.partial(chip_kernel, dims),
        out_shape=(
            jax.ShapeDtypeStruct(block, jnp.bfloat16),
            jax.ShapeDtypeStruct(block, jnp.bfloat16),
            jax.ShapeDtypeStruct((2, ROWS, 128), jnp.bfloat16),
        ),
        in_specs=[hbm, hbm, hbm, hbm, hbm],
        out_specs=(vmem, vmem, vmem),
        scratch_shapes=[
            pltpu.SMEM(clip_lengths.shape, jnp.int32),
            pltpu.VMEM((1, 128), jnp.float32),
            pltpu.VMEM((4, 18, 32, 128), jnp.bfloat16),
            pltpu.VMEM((128, 512), jnp.float32),
            pltpu.VMEM((3, 3 * HALF, 1024), jnp.bfloat16),
            pltpu.VMEM((4, 18, 32, 128), jnp.bfloat16),
            pltpu.VMEM((3, 3, 3, 128, 128), jnp.bfloat16),
            pltpu.VMEM((2, 8, 32, 128), jnp.bfloat16),
            pltpu.VMEM((2, 256, 384), jnp.float32),
            pltpu.VMEM((ROWS, 128), jnp.bfloat16),
            pltpu.VMEM((p_n - 1, chunk, 128), jnp.bfloat16),
            pltpu.VMEM((chunk, 128), jnp.bfloat16),
            pltpu.VMEM((z_n - 1, chunk, 128), jnp.bfloat16),
            pltpu.SemaphoreType.REGULAR((len(rounds_of(z_n)),)),
            pltpu.SemaphoreType.REGULAR((2,)),
            dma((5,)), dma((6,)), dma((6,)), dma((4,)), dma((4,)),
            dma, dma, dma, dma, dma, dma, dma, dma((p_n,)), dma, dma,
        ],
        compiler_params=pltpu.CompilerParams(
            collective_id=0, has_side_effects=True, vmem_limit_bytes=40 * 1024 * 1024
        ),
        name="chip_kernel",
    )(*(pltpu.with_memory_space_constraint(a, pltpu.HBM) for a in operands))
    result, in_grad, kern_grad, bias_grad = pl.pallas_call(
        functools.partial(finish_kernel, p_n),
        out_shape=(
            jax.ShapeDtypeStruct(block, jnp.bfloat16),
            jax.ShapeDtypeStruct(block, jnp.bfloat16),
            jax.ShapeDtypeStruct((3, 3, 3, 128, 128), jnp.float32),
            jax.ShapeDtypeStruct((1, 128), jnp.float32),
        ),
        in_specs=[vmem, vmem, vmem],
        out_specs=(hbm, hbm, hbm, hbm),
        scratch_shapes=[
            pltpu.VMEM((3, 3, 3, 128, 128), jnp.float32),
            pltpu.VMEM((1, 128), jnp.float32),
            dma((12,)),
        ],
        compiler_params=pltpu.CompilerParams(vmem_limit_bytes=32 * 1024 * 1024),
        name="finish_kernel",
    )(result, in_grad, full)
    return result, in_grad, kern_grad, bias_grad.reshape(128)


def solution(mesh):
    dims = (mesh.shape["dp"], mesh.shape["tm"])
    return jax.shard_map(
        functools.partial(on_device, dims),
        mesh=mesh,
        in_specs=(
            P("dp", "tm", "space", None, None),
            P("dp", None),
            P(),
            P(),
            P("dp", "tm", "space", None, None),
        ),
        out_specs=(
            P("dp", "tm", "space", None, None),
            P("dp", "tm", "space", None, None),
            P(),
            P(),
        ),
        check_vma=False,
    )
```

```python
import functools

import jax
import jax.numpy as jnp
from jax import lax
from jax.experimental import pallas as pl
from jax.experimental.pallas import tpu as pltpu
from jax.sharding import PartitionSpec as P

MESH = pl.DeviceIdType.MESH
Z_LO = 4
PLANE_Y = 4
HALF = 64
ROWS = 28 * HALF
TILES = 9 * HALF // 16


def tile_row(p_n, k, tile):
    chunk, per = ROWS // p_n, TILES // p_n
    if k < 3 and tile < per * p_n:
        return tile // per * chunk + (k * per + tile % per) * 16
    extra = k * (TILES - per * p_n) + (tile - per * p_n if k < 3 else tile)
    return extra % p_n * chunk + (3 * per + extra // p_n) * 16


def scalar_mask(ends, frame, lag):
    def clip(t):
        return sum((t >= end).astype(jnp.int32) for end in ends)

    earlier = frame - lag
    same = (clip(earlier) == clip(frame)) & (earlier >= 0)
    return same.astype(jnp.float32)


def scaled(values, mask):
    return values * jnp.full(values.shape, mask, jnp.float32).astype(values.dtype)


def column_sum(parts, back):
    count = parts.shape[0]
    col = lax.broadcasted_iota(jnp.int32, (count, 128), 0) % 32
    first, mid, last = parts[:, :128], parts[:, 128:256], parts[:, 256:]
    down, up = (last, first) if back else (first, last)
    down = jnp.where(col == 0, 0.0, pltpu.roll(down, 1, 0))
    up = jnp.where(col == 31, 0.0, pltpu.roll(up, count - 1, 0))
    return mid + down + up


def chip_kernel(
    dims, lens_hbm, x_hbm, w_hbm, bias_hbm, cot_hbm,
    out_ref, ig_ref, full,
    lens, bias, xs, xt, lt, dzs, wv, cotv, yacc, part, rsbuf, zs, zbuf,
    known, plane_known, loc, xsend, xrecv, dsend, drecv, rs_send, rs_recv, z_send, z_recv,
    zg_send, zg_recv, pg_send, pg_recv, cg_send, cg_recv,
):
    zh_n, tm_n = dims
    z_n, p_n = zh_n * Z_LO, tm_n // Z_LO
    chunk = ROWS // p_n
    rounds = rounds_of(z_n)

    dp, tm, core = lax.axis_index("dp"), lax.axis_index("tm"), lax.axis_index("space")
    other = 1 - core
    p, zl = tm // Z_LO, tm % Z_LO
    z = dp * Z_LO + zl
    after, before = (tm + 1) % tm_n, (tm + tm_n - 1) % tm_n

    def plane_dev(q):
        return (dp, q * Z_LO + zl, core)

    def z_dev(w):
        return (w // Z_LO, p * Z_LO + w % Z_LO, core)

    x_n = p_n // PLANE_Y
    xq = [(p // PLANE_Y + dx) % x_n * PLANE_Y for dx in range(x_n)]
    yq = [(p % PLANE_Y + dy) % PLANE_Y for dy in range(PLANE_Y)]
    far_first = sorted(
        ((dx, dy) for dx in range(x_n) for dy in range(PLANE_Y) if dx + dy),
        key=lambda d: -min(d[0], x_n - d[0]) - min(d[1], PLANE_Y - d[1]),
    )
    next_to = [xq[dx] + yq[0] for dx in (1, x_n - 1) if x_n > 1] + [xq[0] + yq[dy] for dy in (1, PLANE_Y - 1)]
    two_off = [xq[dx] + yq[0] for dx in range(2, x_n, x_n)] + [xq[0] + yq[dy] for dy in range(2, PLANE_Y, PLANE_Y)]

    barrier = pltpu.get_barrier_semaphore()

    def greet(device):
        pl.semaphore_signal(barrier, inc=1, device_id=device, device_id_type=MESH)

    def remote(src, dst, send, recv, device):
        return pltpu.make_async_remote_copy(
            src_ref=src, dst_ref=dst, send_sem=send, recv_sem=recv, device_id=device, device_id_type=MESH
        )

    own = pl.ds(1 + 8 * core, 8)
    edge_row = 7 * other
    edge = pl.ds(1 + 8 * core + edge_row, 1)
    inner = pl.ds(1 + 9 * core, 7)
    two, later = pl.ds(0, 2), pl.ds(2, 2)

    greet((dp, tm, other))
    for there, near in ((tm > 0, before), (tm < tm_n - 1, after)):
        @pl.when(there)
        def _():
            greet((dp, near, core))
            greet((dp, near, other))

    for q in next_to:
        greet(plane_dev(q))
    greet(z_dev((z + 1) % z_n))
    greet(z_dev((z + z_n - 1) % z_n))

    get_x = pltpu.make_async_copy(x_hbm.at[0], xs.at[later, own], loc.at[0])
    get_w = pltpu.make_async_copy(w_hbm, wv, loc.at[1])
    get_cot = pltpu.make_async_copy(cot_hbm.at[0], cotv, loc.at[2])
    get_lens = pltpu.make_async_copy(lens_hbm, lens, loc.at[3])
    get_bias = pltpu.make_async_copy(bias_hbm, bias, loc.at[4])
    for copy in (get_x, get_w, get_lens, get_cot, get_bias):
        copy.start()
    for f in range(4):
        for r in (0, 17):
            xs[f, r] = jnp.zeros((32, 128), jnp.bfloat16)
            dzs[f, r] = jnp.zeros((32, 128), jnp.bfloat16)

    @pl.when(tm == 0)
    def _():
        xs[two, pl.ds(1, 16)] = jnp.zeros((2, 16, 32, 128), jnp.bfloat16)

    @pl.when(tm == tm_n - 1)
    def _():
        dzs[later, pl.ds(1, 16)] = jnp.zeros((2, 16, 32, 128), jnp.bfloat16)

    get_lens.wait()
    ends = [lens[0, 0]]
    for j in range(1, lens.shape[1]):
        ends.append(ends[-1] + lens[0, j])
    base = 2 * tm
    m0 = [scalar_mask(ends, base + t, 2) for t in range(4)]
    m1 = [scalar_mask(ends, base + t, 1) for t in range(3)]

    get_x.wait()
    sides = (tm + tm_n - 1) // tm_n + (2 * (tm_n - 1) - tm) // tm_n
    pl.semaphore_wait(barrier, 1 + len(next_to) + 2 + 2 * sides)

    def tell_plane(r):
        for q in (next_to, two_off)[r]:
            pl.semaphore_signal(plane_known.at[r], inc=1, device_id=plane_dev(q), device_id_type=MESH)

    def hear_plane(r):
        if (next_to, two_off)[r]:
            pl.semaphore_wait(plane_known.at[r], len((next_to, two_off)[r]))

    def tell(r):
        for w in (z + rounds[r], z + z_n - rounds[r]):
            pl.semaphore_signal(known.at[r], inc=1, device_id=z_dev(w % z_n), device_id_type=MESH)

    def hear(r):
        pl.semaphore_wait(known.at[r], 2)

    tell_plane(0)
    tell(0)

    x_next = [
        remote(xs.at[2 + f, own], xs.at[f, own], xsend.at[1 + 4 * f], xrecv.at[1 + 4 * f], (dp, after, core))
        for f in range(2)
    ]
    x_edge = remote(
        xs.at[later, edge], xs.at[two, edge], xsend.at[2], xrecv.at[2], (dp, after, other)
    )
    x_pair = remote(xs.at[later, own], xs.at[later, own], xsend.at[0], xrecv.at[0], (dp, tm, other))
    x_fwd = [
        remote(xs.at[f, inner], xs.at[f, inner], xsend.at[3 + f], xrecv.at[3 + f], (dp, tm, other))
        for f in range(2)
    ]

    @pl.when(tm < tm_n - 1)
    def _():
        x_edge.start()
        x_next[1].start()
        x_next[0].start()

    x_pair.start()

    def x_rows(f):
        return jnp.concatenate(
            [xs[f, pl.ds(8 * core + a, 8)].reshape(256, 128) for a in range(3)], axis=1
        )

    def w_fwd(k):
        return jnp.concatenate(
            [jnp.concatenate([wv[k, a, b] for b in range(3)], axis=1) for a in range(3)], axis=0
        )

    def mm(lhs, rhs):
        return jnp.dot(lhs, rhs, preferred_element_type=jnp.float32)

    def turned(f):
        xt[...] = xs[f, pl.ds(1, 16)].reshape(512, 128).astype(jnp.float32).T
        mid = xt[pl.ds(pl.multiple_of(HALF * core, HALF), HALF), :]
        col = lax.broadcasted_iota(jnp.int32, (HALF, 512), 1) % 32
        left = jnp.where(col == 0, 0.0, pltpu.roll(mid, 1, 1))
        right = jnp.where(col == 31, 0.0, pltpu.roll(mid, 511, 1))
        block = jnp.concatenate([left, mid, right], axis=0)
        for t in range(2):
            k = f - t
            if k < 0 or k > 2:
                continue
            kept = block if k == 2 else block * (m1[t] if k == 1 else m0[t])
            lt[k, :, pl.ds(512 * t, 512)] = kept.astype(jnp.bfloat16)

    get_w.wait()
    x_pair.wait_recv()
    yacc[0] = mm(x_rows(2), w_fwd(2))
    yacc[1] = mm(
        jnp.concatenate([x_rows(3), scaled(x_rows(2), m1[1])], axis=1),
        jnp.concatenate([w_fwd(2), w_fwd(1)], axis=0),
    )
    turned(2)
    turned(3)
    get_cot.wait()
    get_bias.wait()

    def halo_frame(f):
        @pl.when(tm > 0)
        def _():
            x_next[f].wait_recv()
            x_fwd[f].start()

    def finish_frame(f):
        zed = column_sum(yacc[f], False) + bias[...]
        sig = jax.nn.sigmoid(zed)
        out_ref[0, f] = (zed * sig).astype(jnp.bfloat16).reshape(8, 32, 128)
        cot = cotv[f].reshape(256, 128).astype(jnp.float32)
        dz = (cot * sig * (1.0 + zed * (1.0 - sig))).astype(jnp.bfloat16)
        dzs[f, own] = dz.reshape(8, 32, 128)
        d_pair[f].start()
        return jnp.sum(dz.astype(jnp.float32).reshape(16, 16, 128), axis=0)

    d_pair = [
        remote(dzs.at[f, own], dzs.at[f, own], dsend.at[3 * f], drecv.at[3 * f], (dp, tm, other))
        for f in range(2)
    ]

    hear_plane(0)
    tell_plane(1)
    pl.when(tm > 0)(x_edge.wait_recv)
    halo_frame(1)
    yacc[0] += mm(scaled(x_rows(1), m1[0]), w_fwd(1))
    yacc[1] += mm(scaled(x_rows(1), m0[1]), w_fwd(0))
    bias_part = finish_frame(1)
    halo_frame(0)
    yacc[0] += mm(scaled(x_rows(0), m0[0]), w_fwd(0))
    bias_part += finish_frame(0)

    d_next = remote(dzs.at[two, own], dzs.at[later, own], dsend.at[1], drecv.at[1], (dp, before, core))
    d_edge = remote(dzs.at[two, edge], dzs.at[later, edge], dsend.at[2], drecv.at[2], (dp, before, other))

    early, middle = dp < zh_n // 2, dp == zh_n // 2
    near = zl > 0

    def d_start():
        d_next.start()
        d_edge.start()

    pl.when(near | (early & (tm > 0)))(d_start)

    part[pl.ds(tile_row(p_n, 3, 0), 16), :] = bias_part.astype(jnp.bfloat16)
    for spare in range(1, ROWS // 16 - 3 * TILES):
        part[pl.ds(tile_row(p_n, 3, spare), 16), :] = jnp.zeros((16, 128), jnp.bfloat16)
    for f in (1, 0):
        pl.when(tm > 0)(x_fwd[f].wait_recv)
        turned(f)
    d_pair[1].wait_recv()
    d_pair[0].wait_recv()

    right_side = jnp.concatenate(
        [
            jnp.concatenate([dzs[t, pl.ds(2 - a, 16)].reshape(512, 128) for a in range(3)], axis=1)
            for t in range(2)
        ],
        axis=0,
    )

    def chunk_rows(q):
        return pl.ds(pl.multiple_of(q * chunk, 16), chunk)

    per = TILES // p_n * 16
    for k in range(3):
        grad = mm(lt[k], right_side)
        for a in range(3):
            for b in range(3):
                for j in range(HALF // 16):
                    block = grad[b * HALF + j * 16 : b * HALF + j * 16 + 16, a * 128 : (a + 1) * 128]
                    row = tile_row(p_n, k, (a * 3 + b) * (HALF // 16) + j)
                    part[pl.ds(row, 16), :] = block.astype(jnp.bfloat16)
        count = per if k < 2 else chunk - 2 * per
        if k == 0:
            hear_plane(1)

        for dx, dy in far_first:
            q = xq[dx] + yq[dy]
            remote(
                part.at[pl.ds(pl.multiple_of(q * chunk + k * per, 16), count)],
                rsbuf.at[dx * PLANE_Y + dy - 1, pl.ds(k * per, count)], rs_send, rs_recv, plane_dev(q),
            ).start()

    hear(0)
    if len(rounds) > 1:
        tell(1)

    def d_rows(f):
        return jnp.concatenate(
            [dzs[f, pl.ds(8 * core + 2 - a, 8)].reshape(256, 128) for a in range(3)], axis=1
        )

    def w_back(k):
        return jnp.concatenate([wv[k, a].reshape(384, 128) for a in range(3)], axis=1)

    def mm_t(lhs, rhs):
        return lax.dot_general(lhs, rhs, (((1,), (1,)), ((), ())), preferred_element_type=jnp.float32)

    yacc[0] = mm_t(
        jnp.concatenate([d_rows(0), scaled(d_rows(1), m1[1])], axis=1),
        jnp.concatenate([w_back(2), w_back(1)], axis=1),
    )
    yacc[1] = mm_t(d_rows(1), w_back(2))

    for r in range(1, len(rounds) - 1):
        hear(r)
        tell(r + 1)

    remote(rsbuf, rsbuf, rs_send, rs_recv, plane_dev(p)).wait_recv()
    total = part[chunk_rows(p), :].astype(jnp.float32)
    for q in range(p_n - 1):
        total += rsbuf[q].astype(jnp.float32)
    zs[...] = total.astype(jnp.bfloat16)

    if len(rounds) > 1:
        hear(len(rounds) - 1)

    to_first = remote(zs, zbuf.at[(z + z_n - 1) % z_n], z_send, z_recv, z_dev(z * 0))
    pl.when(z > 0)(to_first.start)
    pl.when(jnp.logical_not(near) & middle & (tm > 0))(d_start)

    def rest_of_in_grad():
        @pl.when(tm < tm_n - 1)
        def _():
            d_next.wait_recv()
            d_edge.wait_recv()

        yacc[0] += mm_t(scaled(d_rows(2), m0[2]), w_back(0))
        yacc[1] += mm_t(
            jnp.concatenate([scaled(d_rows(2), m1[2]), scaled(d_rows(3), m0[3])], axis=1),
            jnp.concatenate([w_back(1), w_back(0)], axis=1),
        )
        for f in range(2):
            ig_ref[0, f] = column_sum(yacc[f], True).astype(jnp.bfloat16).reshape(8, 32, 128)

    pl.when(early | middle)(rest_of_in_grad)

    half = z_n // 2
    mine = full.at[core, chunk_rows(p)]

    def z_share(w):
        remote(mine, mine, zg_send, zg_recv, z_dev(w)).start()

    @pl.when(z == 0)
    def _():
        shares = zbuf.at[pl.ds(0, z_n - 1)]
        remote(shares, shares, z_send, z_recv, z_dev(z)).wait_recv()
        acc = zs[...].astype(jnp.float32)
        for w in range(z_n - 1):
            acc += zbuf[w].astype(jnp.float32)
        full[core, chunk_rows(p), :] = acc.astype(jnp.bfloat16)
        for w in (*range(1, half), z_n - 1):
            z_share(w)

    pl.when(z > 0)(lambda: remote(mine, mine, zg_send, zg_recv, z_dev(z)).wait_recv())

    @pl.when(z == z_n - 1)
    def _():
        for w in range(half, z_n - 1):
            z_share(w)

    for dx, dy in far_first:
        remote(mine, mine, pg_send, pg_recv.at[p], plane_dev(xq[dx] + yq[dy])).start()


    pl.when(jnp.logical_not(near | early | middle) & (tm > 0))(d_start)

    def cg_copy(rows):
        return remote(full.at[core, rows], full.at[core, rows], cg_send, cg_recv, (dp, tm, other))

    cg_copy(chunk_rows(p)).start()

    @pl.loop(1, p_n)
    def _(i):
        q = (p + i) % p_n
        rows = chunk_rows(q)
        remote(full.at[core, rows], full.at[core, rows], pg_send, pg_recv.at[q], plane_dev(q)).wait_recv()
        cg_copy(rows).start()

    pl.when(jnp.logical_not(early | middle))(rest_of_in_grad)

    @pl.when(tm < tm_n - 1)
    def _():
        x_next[0].wait_send()
        x_next[1].wait_send()
        x_edge.wait_send()

    x_pair.wait_send()
    d_pair[0].wait_send()
    d_pair[1].wait_send()

    @pl.when(tm > 0)
    def _():
        x_fwd[0].wait_send()
        x_fwd[1].wait_send()
        d_next.wait_send()
        d_edge.wait_send()

    rest = pl.ds(0, (p_n - 1) * chunk)
    remote(part.at[rest], part.at[rest], rs_send, rs_recv, plane_dev(p)).wait_send()

    pl.when(z > 0)(to_first.wait_send)
    for w, count in ((0, half), (z_n - 1, half - 1)):
        if count:
            sent = zbuf.at[pl.ds(0, count)]
            pl.when(z == w)(remote(sent, sent, zg_send, z_recv, z_dev(z)).wait_send)

    remote(full.at[core, rest], full.at[core, rest], pg_send, pg_recv.at[p], plane_dev(p)).wait_send()
    everything = remote(full.at[core], full.at[other], cg_send, cg_recv, (dp, tm, other))
    everything.wait_send()
    everything.wait_recv()


def finish_kernel(p_n, out_in, ig_in, full, out_ref, ig_ref, grad_ref, bias_ref, buf, bias_buf, sems):
    copies = [
        pltpu.make_async_copy(out_in, out_ref, sems.at[0]),
        pltpu.make_async_copy(ig_in, ig_ref, sems.at[1]),
    ]
    for k in range(3):
        for a in range(3):
            for b in range(3):
                for side in range(2):
                    for j in range(HALF // 16):
                        row = tile_row(p_n, k, (a * 3 + b) * (HALF // 16) + j)
                        buf[k, a, b, pl.ds(side * HALF + j * 16, 16), :] = full[
                            side, pl.ds(row, 16), :
                        ].astype(jnp.float32)
            copies.append(pltpu.make_async_copy(buf.at[k, a], grad_ref.at[k, a], sems.at[3 + 3 * k + a]))
            copies[-1].start()
    copies[0].start()
    copies[1].start()
    terms = full[:, pl.ds(tile_row(p_n, 3, 0), 16), :].astype(jnp.float32)
    bias_buf[...] = jnp.sum(terms[0] + terms[1], axis=0, keepdims=True)
    copies.append(pltpu.make_async_copy(bias_buf, bias_ref, sems.at[2]))
    copies[-1].start()
    for copy in copies:
        copy.wait()


def rounds_of(z_n):
    rounds = [1]
    while 2 * rounds[-1] < z_n // 2:
        rounds.append(2 * rounds[-1])
    return rounds


def on_device(dims, inputs, clip_lengths, weight, bias, cotangent):
    zh_n, tm_n = dims
    z_n, p_n = zh_n * Z_LO, tm_n // Z_LO
    chunk = ROWS // p_n
    block = inputs.shape
    dma = pltpu.SemaphoreType.DMA
    vmem, hbm = (pl.BlockSpec(memory_space=m) for m in (pltpu.VMEM, pltpu.HBM))
    operands = (clip_lengths, inputs, weight, bias.reshape(1, 128), cotangent)
    result, in_grad, full = pl.pallas_call(
        functools.partial(chip_kernel, dims),
        out_shape=(
            jax.ShapeDtypeStruct(block, jnp.bfloat16),
            jax.ShapeDtypeStruct(block, jnp.bfloat16),
            jax.ShapeDtypeStruct((2, ROWS, 128), jnp.bfloat16),
        ),
        in_specs=[hbm, hbm, hbm, hbm, hbm],
        out_specs=(vmem, vmem, vmem),
        scratch_shapes=[
            pltpu.SMEM(clip_lengths.shape, jnp.int32),
            pltpu.VMEM((1, 128), jnp.float32),
            pltpu.VMEM((4, 18, 32, 128), jnp.bfloat16),
            pltpu.VMEM((128, 512), jnp.float32),
            pltpu.VMEM((3, 3 * HALF, 1024), jnp.bfloat16),
            pltpu.VMEM((4, 18, 32, 128), jnp.bfloat16),
            pltpu.VMEM((3, 3, 3, 128, 128), jnp.bfloat16),
            pltpu.VMEM((2, 8, 32, 128), jnp.bfloat16),
            pltpu.VMEM((2, 256, 384), jnp.float32),
            pltpu.VMEM((ROWS, 128), jnp.bfloat16),
            pltpu.VMEM((p_n - 1, chunk, 128), jnp.bfloat16),
            pltpu.VMEM((chunk, 128), jnp.bfloat16),
            pltpu.VMEM((z_n, chunk, 128), jnp.bfloat16),
            pltpu.SemaphoreType.REGULAR((len(rounds_of(z_n)),)),
            pltpu.SemaphoreType.REGULAR((2,)),
            dma((5,)), dma((6,)), dma((6,)), dma((4,)), dma((4,)),
            dma, dma, dma, dma, dma, dma, dma, dma((p_n,)), dma, dma,
        ],
        compiler_params=pltpu.CompilerParams(
            collective_id=0, has_side_effects=True, vmem_limit_bytes=40 * 1024 * 1024
        ),
        name="chip_kernel",
    )(*(pltpu.with_memory_space_constraint(a, pltpu.HBM) for a in operands))
    result, in_grad, kern_grad, bias_grad = pl.pallas_call(
        functools.partial(finish_kernel, p_n),
        out_shape=(
            jax.ShapeDtypeStruct(block, jnp.bfloat16),
            jax.ShapeDtypeStruct(block, jnp.bfloat16),
            jax.ShapeDtypeStruct((3, 3, 3, 128, 128), jnp.float32),
            jax.ShapeDtypeStruct((1, 128), jnp.float32),
        ),
        in_specs=[vmem, vmem, vmem],
        out_specs=(hbm, hbm, hbm, hbm),
        scratch_shapes=[
            pltpu.VMEM((3, 3, 3, 128, 128), jnp.float32),
            pltpu.VMEM((1, 128), jnp.float32),
            dma((12,)),
        ],
        compiler_params=pltpu.CompilerParams(vmem_limit_bytes=32 * 1024 * 1024),
        name="finish_kernel",
    )(result, in_grad, full)
    return result, in_grad, kern_grad, bias_grad.reshape(128)


def solution(mesh):
    dims = (mesh.shape["dp"], mesh.shape["tm"])
    return jax.shard_map(
        functools.partial(on_device, dims),
        mesh=mesh,
        in_specs=(
            P("dp", "tm", "space", None, None),
            P("dp", None),
            P(),
            P(),
            P("dp", "tm", "space", None, None),
        ),
        out_specs=(
            P("dp", "tm", "space", None, None),
            P("dp", "tm", "space", None, None),
            P(),
            P(),
        ),
        check_vma=False,
    )
```
